512 devices in a mesh: dp: 16 (over x, z_hi), rows: 32 (over y, z_lo, core).
Axes of the slice: x: 4, y: 4, z: 16 (z_hi: 4, z_lo: 4; z = z_hi * 4 + z_lo), core: 2. Of those that a mesh axis runs over, the one named last changes fastest.
Arguments:
- cotangent: bfloat16 [64, 64, 128, 128], P('dp', 'rows'), may hold values from -6 to 6
- inputs: bfloat16 [16, 128, 64, 256], P('dp', 'rows'), may hold values from -6 to 6
- w_first: bfloat16 [3, 3, 256, 256], replicated, may hold values from -0.125 to 0.125
- bias_first: float32 [256], replicated, may hold values from -3 to 3
- w_second: bfloat16 [3, 3, 256, 128], replicated, may hold values from -0.125 to 0.125
Outputs:
- grad_input: bfloat16 [16, 128, 64, 256], P('dp', 'rows')
- grad_w_first: float32 [2304, 256], P('dp')
- grad_w_second: float32 [2304, 128], P('dp')
- grad_bias: float32 [256], P('dp')
The draws below stay inside these ranges and needn't reach their ends.
All inputs are finite; a program needn't handle non-finite values.
Results may differ from the reference program's by a relative error of at most 0.0075.
Values may be sent and summed in bfloat16 or wider, within the bound.
No kernel may reach another device: no remote copies, remote signals or barrier semaphores. Data moves between devices by JAX's collectives and lax.ppermute only.
A program may use at most 64 MiB of HBM per device.

```python
import jax
import jax.numpy as jnp
from jax import lax

C1 = 256
C2 = 128
IMGS = 4
ROWS_DEV = 2
W_LO = 64
W_HI = 128
BATCH = 64
H_LO = 32
H_HI = 64
PIX_LO = 131072
PIX_HI = 524288
N_DP = 16
N_ROWS = 32


def levels(stream_key, extent, pieces, smallest, largest):
    def one(axis_at, shards_of):
        draws = jax.random.uniform(jax.random.fold_in(jax.random.fold_in(stream_key, 6), axis_at), (shards_of,), jnp.float32, smallest / len(pieces), largest / len(pieces))
        return jnp.repeat(jnp.exp(draws), extent[axis_at] // shards_of).reshape((-1,) + (1,) * (len(extent) - axis_at - 1))

    gain = one(*pieces[0])
    for cut in pieces[1:]:
        gain = gain * one(*cut)
    return gain


def normal_values(key, dims, spread, bound, pieces=(), dtype=jnp.bfloat16):
    entries = jax.random.normal(key, dims, jnp.float32) * spread
    if len(pieces) > 0:
        entries = levels(key, dims, pieces, -0.22, 0.18) * entries
    return jnp.clip(entries, min=-bound, max=bound).astype(dtype)


def setup_inputs(seed: int = 0) -> dict:
    arg_keys = jax.random.split(jax.random.key(seed), 6)
    cotangent = normal_values(arg_keys[0], (BATCH, H_HI, W_HI, C2), 1.0, 6.0, ((0, 16), (1, 32)))
    inputs = normal_values(arg_keys[1], (N_DP, 2 * ROWS_DEV * N_ROWS, W_LO, C1), 1.0, 6.0, ((0, 16), (1, 32)))
    w_first = normal_values(arg_keys[2], (3, 3, C1, C1), (9 * C1) ** -0.5, 0.125)
    bias_first = normal_values(arg_keys[3], (C1,), 0.5, 3.0, (), jnp.float32)
    w_second = normal_values(arg_keys[4], (3, 3, C1, C2), (9 * C1) ** -0.5, 0.125)
    return dict(cotangent=cotangent, inputs=inputs, w_first=w_first, bias_first=bias_first, w_second=w_second)


def pad_columns(values):
    return jnp.pad(values, ((0, 0), (1, 1), (1, 1), (0, 0)))

def conv_apply(padded, weight):
    rows_out = padded.shape[1] - 2
    cols_out = padded.shape[2] - 2
    chan_in = padded.shape[3]
    total = jnp.zeros((padded.shape[0] * rows_out * cols_out, weight.shape[3]), jnp.float32)
    for offset_y in range(3):
        for offset_x in range(3):
            window = padded[:, offset_y:offset_y + rows_out, offset_x:offset_x + cols_out].reshape(-1, chan_in)
            total = total + jnp.dot(window, weight[offset_y, offset_x], preferred_element_type=jnp.float32)
    return total.reshape(padded.shape[0], rows_out, cols_out, weight.shape[3])

def conv_adjoint(padded, weight):
    return conv_apply(padded, jnp.transpose(weight[::-1, ::-1], (0, 1, 3, 2)))

def weight_grad(padded, gradient):
    rows_out = gradient.shape[1]
    cols_out = gradient.shape[2]
    chan_in = padded.shape[3]
    flat_grad = gradient.reshape(-1, gradient.shape[3])
    taps = []
    for offset_y in range(3):
        for offset_x in range(3):
            window = padded[:, offset_y:offset_y + rows_out, offset_x:offset_x + cols_out].reshape(-1, chan_in)
            taps.append(lax.dot_general(window, flat_grad, (((0,), (0,)), ((), ())), preferred_element_type=jnp.float32))
    return jnp.stack(taps).reshape(3, 3, chan_in, gradient.shape[3])

def silu_slope(preact):
    sigma = jax.nn.sigmoid(preact)
    return sigma * (1.0 + preact * (1.0 - sigma))

def reference(cotangent, inputs, w_first, bias_first, w_second):
    images = inputs.reshape(N_DP, N_ROWS // 4, IMGS, 2 * ROWS_DEV, W_LO, C1)
    images = images.transpose(0, 2, 1, 3, 4, 5).reshape(BATCH, H_LO, W_LO, C1)

    def one_image(running, sample):
        image, grad_out = sample
        padded_in = pad_columns(image[None])
        preact = conv_apply(padded_in, w_first) + bias_first
        activation = jax.nn.silu(preact).astype(jnp.bfloat16)
        upsampled = jnp.repeat(jnp.repeat(activation, 2, axis=1), 2, axis=2)
        grad_up = conv_adjoint(pad_columns(grad_out[None]), w_second)
        raw_second = weight_grad(pad_columns(upsampled), grad_out[None])
        grad_act = grad_up.reshape(1, H_LO, 2, W_LO, 2, C1).sum(axis=(2, 4))
        delta = (grad_act * silu_slope(preact)).astype(jnp.bfloat16)
        raw_bias = lax.optimization_barrier(jnp.sum(delta.astype(jnp.float32), axis=(0, 1, 2)))
        raw_first = weight_grad(padded_in, delta)
        grad_image = conv_adjoint(pad_columns(delta), w_first).astype(jnp.bfloat16)
        return ((running[0] + raw_first, running[1] + raw_second, running[2] + raw_bias), grad_image[0])
    start = (jnp.zeros((3, 3, C1, C1), jnp.float32), jnp.zeros((3, 3, C1, C2), jnp.float32), jnp.zeros((C1,), jnp.float32))
    totals, grad_images = lax.scan(one_image, start, (images, cotangent))
    grad_input = grad_images.reshape(N_DP, IMGS, N_ROWS // 4, 2 * ROWS_DEV, W_LO, C1)
    grad_input = grad_input.transpose(0, 2, 1, 3, 4, 5).reshape(N_DP, 2 * ROWS_DEV * N_ROWS, W_LO, C1)
    scale_low = PIX_LO ** (-0.5)
    scale_high = PIX_HI ** (-0.5)
    grad_w_first = totals[0].reshape(9 * C1, C1) * scale_low
    grad_w_second = totals[1].reshape(9 * C1, C2) * scale_high
    grad_bias = totals[2] * scale_low
    return (grad_input, grad_w_first, grad_w_second, grad_bias)
```

```python
import jax
import jax.numpy as jnp
from jax import lax
from jax.experimental import pallas as pl
from jax.experimental.pallas import tpu as pltpu
from jax.sharding import PartitionSpec as P

F32 = jnp.float32
BF16 = jnp.bfloat16
COLS = 64
C1 = 256
C2 = 128
ROWS = 4
PIX = ROWS * COLS
SLICE = 144
PACK = 448
HALF = PACK // 2


def dot(a, b, contract):
    return lax.dot_general(a, b, (contract, ((), ())), preferred_element_type=F32)


NN = ((1,), (0,))
NT = ((1,), (1,))
TN = ((0,), (0,))


def shifted(value, by):
    length = value.shape[0]
    column = lax.broadcasted_iota(jnp.int32, value.shape, 0) % COLS
    rolled = pltpu.roll(value, (-by) % length, 0)
    inside = (column + by >= 0) & (column + by < COLS)
    return jnp.where(inside, rolled, 0.0)


def put(packed, band, tap, value):
    first = tap * C1
    row = 0
    while row < C1:
        d, inner = divmod(first + row, SLICE)
        place = band * SLICE + inner
        count = min(C1 - row, SLICE - inner, HALF - place % HALF)
        half, place = divmod(place, HALF)
        packed[half, d, place : place + count, :] = value[row : row + count, :]
        row += count


def body(
    core, x, above, below, cot, w1, bias, w2,
    grad_x, edge_up, edge_down, keep, send,
    xs, cpad, boxes, ds, packed, sems,
):
    xs[1, 0:COLS, 0:C2] = above[1, 0:COLS, :]
    xs[1, 0:COLS, C2:C1] = above[1, COLS : 2 * COLS, :]
    xs[1, COLS : COLS + PIX, :] = x[...]
    xs[1, COLS + PIX :, 0:C2] = below[1, 0:COLS, :]
    xs[1, COLS + PIX :, C2:C1] = below[1, COLS : 2 * COLS, :]
    wide = xs[1].astype(F32)
    xs[0] = shifted(wide, -1).astype(BF16)
    xs[2] = shifted(wide, 1).astype(BF16)

    preact = jnp.broadcast_to(bias[...], (PIX, C1))
    for p in range(3):
        for q in range(3):
            preact = preact + dot(xs[q, p * COLS : p * COLS + PIX, :], w1[3 * p + q], NN)
    sigma = 1.0 / (1.0 + jnp.exp(-preact))
    act = (preact * sigma).astype(BF16)
    slope = sigma * (1.0 + preact * (1.0 - sigma))

    cpad[0:128, :] = above[0]
    cpad[128 : 128 * 9, :] = cot[...]
    cpad[128 * 9 :, :] = below[0]
    out_row = lax.broadcasted_iota(jnp.int32, (3 * COLS, 256), 0)
    column = lax.broadcasted_iota(jnp.int32, (3 * COLS, 256), 1) % 128
    left = 2 * (out_row % COLS) + 1 - out_row // COLS
    pick = ((column == left) | (column == left + 1)).astype(F32).astype(BF16)
    for h in range(-1, 8):
        sums = dot(pick, cpad[128 * (h + 1) : 128 * (h + 3), :], NN).astype(BF16)
        for p in range(3):
            if (h + p - 1) % 2 == 0 and 0 <= (h + p - 1) // 2 < ROWS:
                i = (h + p - 1) // 2
                for q in range(3):
                    t = 3 * p + q
                    boxes[COLS * i : COLS * (i + 1), C2 * t : C2 * (t + 1)] = sums[
                        COLS * q : COLS * (q + 1), :
                    ]
    grad_act = jnp.zeros((PIX, C1), F32)
    for t in range(9):
        grad_act = grad_act + dot(boxes[:, C2 * t : C2 * (t + 1)], w2[t], NT)
    second = dot(act, boxes[...], TN).astype(BF16)
    for t in range(9):
        put(packed, 2, t, second[:, C2 * t : C2 * (t + 1)])

    delta = (grad_act * slope).astype(BF16)
    wide = delta.astype(F32)
    ds[0] = shifted(wide, 1).astype(BF16)
    ds[1] = delta
    ds[2] = shifted(wide, -1).astype(BF16)

    total = jnp.sum(wide, axis=0, keepdims=True).astype(BF16).astype(F32)
    owner = lax.broadcasted_iota(jnp.int32, (16, C1), 0)
    channel = lax.broadcasted_iota(jnp.int32, (16, C1), 1)
    spread = jnp.where(channel // 16 == owner, jnp.broadcast_to(total, (16, C1)), 0.0)
    source = lax.broadcasted_iota(jnp.int32, (C1, 128), 0)
    lane = lax.broadcasted_iota(jnp.int32, (C1, 128), 1)
    fold = (source % 16 == lane).astype(F32).astype(BF16)
    folded = dot(spread.astype(BF16), fold, NN)
    row = lax.broadcasted_iota(jnp.int32, (16, 16, 128), 1)
    band = jnp.where(row == 0, jnp.broadcast_to(folded[:, None, :], (16, 16, 128)), 0.0)
    packed[1, :, HALF - 16 :, :] = band.astype(BF16)

    for p in range(3):
        lhs = xs[1, p * COLS : p * COLS + PIX, :]
        for q in range(3):
            part = dot(lhs, ds[q], TN).astype(BF16)
            put(packed, 0, 3 * p + q, part[:, 0:C2])
            put(packed, 1, 3 * p + q, part[:, C2:C1])

    mine = core[0]
    keep_copy = pltpu.make_async_copy(packed.at[mine], keep, sems.at[0])
    send_copy = pltpu.make_async_copy(packed.at[1 - mine], send, sems.at[1])
    send_copy.start()
    keep_copy.start()

    parts = []
    for p in range(3):
        part = jnp.zeros((PIX, C1), F32)
        for q in range(3):
            part = part + dot(ds[q], w1[3 * p + q], NT)
        parts.append(part)
    zero = jnp.zeros((COLS, C1), F32)
    rows = [
        sum(
            (parts[p][COLS * (r - p) : COLS * (r - p + 1)] for p in range(3) if 0 <= r - p < ROWS),
            zero,
        )
        for r in range(ROWS + 2)
    ]
    edge_up[...] = rows[0].astype(BF16)
    for r in range(ROWS):
        grad_x[COLS * r : COLS * (r + 1), :] = rows[r + 1].astype(BF16)
    edge_down[...] = rows[ROWS + 1].astype(BF16)
    send_copy.wait()
    keep_copy.wait()


def local_work(core, x, above, below, cot, w1, bias, w2):
    vmem = pl.BlockSpec(memory_space=pltpu.VMEM)
    hbm = pl.BlockSpec(memory_space=pl.ANY)
    return pl.pallas_call(
        body,
        out_shape=(
            jax.ShapeDtypeStruct((PIX, C1), BF16),
            jax.ShapeDtypeStruct((COLS, C1), BF16),
            jax.ShapeDtypeStruct((COLS, C1), BF16),
            jax.ShapeDtypeStruct((16, HALF, 128), BF16),
            jax.ShapeDtypeStruct((16, HALF, 128), BF16),
        ),
        in_specs=[pl.BlockSpec(memory_space=pltpu.SMEM)] + [vmem] * 7,
        out_specs=(vmem, vmem, vmem, hbm, hbm),
        scratch_shapes=[
            pltpu.VMEM((3, PIX + 2 * COLS, C1), BF16),
            pltpu.VMEM((128 * 10, C2), BF16),
            pltpu.VMEM((PIX, 9 * C2), BF16),
            pltpu.VMEM((3, PIX, C1), BF16),
            pltpu.VMEM((2, 16, HALF, 128), BF16),
            pltpu.SemaphoreType.DMA((2,)),
        ],
        compiler_params=pltpu.CompilerParams(vmem_limit_bytes=40 * 2**20),
        cost_estimate=pl.CostEstimate(
            flops=1_600_000_000, bytes_accessed=5_000_000, transcendentals=70_000
        ),
        name="local_work",
    )(core, x, above, below, cot, w1, bias, w2)


FOUR = range(4)


def place(x, z_hi, y, z_lo, core):
    return (x * 4 + z_hi) * 32 + y * 8 + z_lo * 2 + core


PLANE = [
    [place(x, zh, y, zl, c) for x in FOUR for y in FOUR]
    for zh in FOUR
    for zl in FOUR
    for c in range(2)
]
COLUMN = [
    [place(x, zh, y, zl, c) for zh in FOUR for zl in FOUR]
    for x in FOUR
    for y in FOUR
    for c in range(2)
]
SHARE = [[y * 8 + zl * 2 + c for c in range(2) for y in FOUR] for zl in FOUR]
QUADS = [[4 * j + b for b in FOUR] for j in range(8)]


def added(pieces):
    return jnp.sum(pieces.astype(F32), axis=0).astype(BF16)


def shards(cotangent, inputs, w_first, bias_first, w_second):
    rank = lax.axis_index("rows")
    down = [(i, i + 4) for i in range(28)]
    up = [(i + 4, i) for i in range(28)]
    x = inputs[0]

    cot = lax.all_to_all(cotangent, "rows", 0, 0, axis_index_groups=QUADS)
    cot = cot.reshape(8, 128, C2)

    def halo(cot_row, x_row):
        return jnp.stack([cot_row, jnp.concatenate([x_row[:, :C2], x_row[:, C2:]], axis=0)])

    above = lax.ppermute(halo(cot[7], x[3]), "rows", down)
    below = lax.ppermute(halo(cot[0], x[0]), "rows", up)
    core = (rank % 2).astype(jnp.int32).reshape(1)
    grad_x, edge_up, edge_down, keep, send = local_work(
        core,
        x.reshape(PIX, C1),
        above,
        below,
        cot.reshape(8 * 128, C2),
        w_first.reshape(9, C1, C1),
        bias_first.reshape(1, C1),
        w_second.reshape(9, C1, C2),
    )
    received = lax.ppermute(send, "rows", [(i, i ^ 1) for i in range(32)])
    from_above = lax.ppermute(edge_down, "rows", down)
    from_below = lax.ppermute(edge_up, "rows", up)

    pair = (keep.astype(F32) + received.astype(F32)).astype(BF16)
    pair = pair.reshape(4, 4, 4, 56, 128).transpose(0, 2, 1, 3, 4).reshape(16, 4, 56, 128)
    both = ("dp", "rows")
    plane = added(lax.all_to_all(pair, both, 0, 0, axis_index_groups=PLANE))
    spread = jnp.broadcast_to(plane[:, None], (4, 4, 56, 128)).reshape(16, 56, 128)
    piece = added(lax.all_to_all(spread, both, 0, 0, axis_index_groups=COLUMN))
    copies = jnp.broadcast_to(piece[None], (8, 56, 128))
    full = lax.all_to_all(copies, "rows", 0, 0, axis_index_groups=SHARE)
    full = full.reshape(PACK, 128).astype(F32)

    pixels_low = lax.axis_size("dp") * lax.axis_size("rows") * PIX
    scale_low = pixels_low ** (-0.5)
    scale_high = (4 * pixels_low) ** (-0.5)
    grad_first = jnp.concatenate([full[:SLICE], full[SLICE : 2 * SLICE]], axis=1) * scale_low
    grad_second = full[2 * SLICE : 3 * SLICE] * scale_high
    grad_bias = full[3 * SLICE, :16] * scale_low

    zero = jnp.zeros((2, COLS, C1), F32)
    fix = jnp.concatenate([from_above[None].astype(F32), zero, from_below[None].astype(F32)])
    grad_input = (grad_x.reshape(ROWS, COLS, C1).astype(F32) + fix).astype(BF16)
    return grad_input[None], grad_first, grad_second, grad_bias


def solution(mesh):
    in_specs = (P("dp", "rows", None, None), P("dp", "rows", None, None), P(), P(), P())
    out_specs = (P("dp", "rows", None, None), P("dp", None), P("dp", None), P("dp"))
    return jax.shard_map(shards, mesh=mesh, in_specs=in_specs, out_specs=out_specs, check_vma=False)
```

```python
import jax
import jax.numpy as jnp
from jax import lax
from jax.experimental import pallas as pl
from jax.experimental.pallas import tpu as pltpu
from jax.sharding import PartitionSpec as P

F32 = jnp.float32
BF16 = jnp.bfloat16
COLS = 64
C1 = 256
C2 = 128
ROWS = 4
PIX = ROWS * COLS
SLICE = 144
PIECE = 32
PIECES = 16
PACK = PIECE * PIECES


def dot(a, b, contract):
    return lax.dot_general(a, b, (contract, ((), ())), preferred_element_type=F32)


NN = ((1,), (0,))
NT = ((1,), (1,))
TN = ((0,), (0,))


def shifted(value, by):
    length = value.shape[0]
    column = lax.broadcasted_iota(jnp.int32, value.shape, 0) % COLS
    rolled = pltpu.roll(value, (-by) % length, 0)
    inside = (column + by >= 0) & (column + by < COLS)
    return jnp.where(inside, rolled, 0.0)


def spot(d, row):
    piece, inner = divmod(row, PIECE)
    half, rest = divmod(piece, PIECES // 2)
    x, z_hi = divmod(d, 4)
    return half, x * (PIECES // 2) + rest, z_hi, inner


def put(packed, band, tap, value):
    row = 0
    while row < C1:
        d, inner = divmod(tap * C1 + row, SLICE)
        half, chunk, z_hi, at = spot(d, band * SLICE + inner)
        count = min(C1 - row, SLICE - inner, PIECE - at)
        packed[half, chunk, z_hi, at : at + count, :] = value[row : row + count, :]
        row += count


def pick_columns():
    out_row = lax.broadcasted_iota(jnp.int32, (3 * COLS, 256), 0)
    column = lax.broadcasted_iota(jnp.int32, (3 * COLS, 256), 1) % 128
    left = 2 * (out_row % COLS) + 1 - out_row // COLS
    return ((column == left) | (column == left + 1)).astype(F32).astype(BF16)


def silu_parts(preact):
    sigma = 1.0 / (1.0 + jnp.exp(-preact))
    return preact * sigma, sigma * (1.0 + preact * (1.0 - sigma))


def main_body(
    core, above, below, cot, x_hbm, w1_hbm, bias_hbm, w2_hbm,
    delta_out, delta_first, delta_last, keep, send,
    xs, cpad, boxes, ds, packed, x, w1, bias, w2, sems,
):
    w2_copy = pltpu.make_async_copy(w2_hbm, w2, sems.at[2])
    w2_copy.start()
    x_copy = pltpu.make_async_copy(x_hbm, x, sems.at[3])
    x_copy.start()
    bias_copy = pltpu.make_async_copy(bias_hbm, bias, sems.at[4])
    bias_copy.start()
    w1_copy = pltpu.make_async_copy(w1_hbm, w1, sems.at[5])
    w1_copy.start()

    cpad[0:128, :] = above[0]
    cpad[128 : 128 * 9, :] = cot[...]
    cpad[128 * 9 :, :] = below[0]
    pick = pick_columns()
    for h in range(-1, 8):
        sums = dot(pick, cpad[128 * (h + 1) : 128 * (h + 3), :], NN).astype(BF16)
        for p in range(3):
            if (h + p - 1) % 2 == 0 and 0 <= (h + p - 1) // 2 < ROWS:
                i = (h + p - 1) // 2
                for q in range(3):
                    t = 3 * p + q
                    boxes[COLS * i : COLS * (i + 1), C2 * t : C2 * (t + 1)] = sums[
                        COLS * q : COLS * (q + 1), :
                    ]
    w2_copy.wait()
    grad_act = jnp.zeros((PIX, C1), F32)
    for t in range(9):
        grad_act = grad_act + dot(boxes[:, C2 * t : C2 * (t + 1)], w2[t], NT)

    x_copy.wait()
    xs[1, 0:COLS, 0:C2] = above[1, 0:COLS, :]
    xs[1, 0:COLS, C2:C1] = above[1, COLS : 2 * COLS, :]
    xs[1, COLS : COLS + PIX, :] = x[...]
    xs[1, COLS + PIX :, 0:C2] = below[1, 0:COLS, :]
    xs[1, COLS + PIX :, C2:C1] = below[1, COLS : 2 * COLS, :]
    wide = xs[1].astype(F32)
    xs[0] = shifted(wide, -1).astype(BF16)
    xs[2] = shifted(wide, 1).astype(BF16)
    bias_copy.wait()
    w1_copy.wait()
    preact = jnp.broadcast_to(bias[...], (PIX, C1))
    for p in range(3):
        for q in range(3):
            preact = preact + dot(xs[q, p * COLS : p * COLS + PIX, :], w1[3 * p + q], NN)
    act, slope = silu_parts(preact)
    second = dot(act.astype(BF16), boxes[...], TN).astype(BF16)
    for t in range(9):
        put(packed, 2, t, second[:, C2 * t : C2 * (t + 1)])

    delta = (grad_act * slope).astype(BF16)
    delta_out[...] = delta
    delta_first[...] = delta[0:COLS]
    delta_last[...] = delta[PIX - COLS : PIX]
    wide = delta.astype(F32)
    ds[0] = shifted(wide, 1).astype(BF16)
    ds[1] = delta
    ds[2] = shifted(wide, -1).astype(BF16)

    total = jnp.sum(wide, axis=0, keepdims=True).astype(BF16).astype(F32)
    owner = lax.broadcasted_iota(jnp.int32, (16, C1), 0)
    channel = lax.broadcasted_iota(jnp.int32, (16, C1), 1)
    spread = jnp.where(channel // 16 == owner, jnp.broadcast_to(total, (16, C1)), 0.0)
    source = lax.broadcasted_iota(jnp.int32, (C1, 128), 0)
    lane = lax.broadcasted_iota(jnp.int32, (C1, 128), 1)
    fold = (source % 16 == lane).astype(F32).astype(BF16)
    folded = dot(spread.astype(BF16), fold, NN)
    row = lax.broadcasted_iota(jnp.int32, (16, 16, 128), 1)
    band = jnp.where(row == 0, jnp.broadcast_to(folded[:, None, :], (16, 16, 128)), 0.0)
    band = band.astype(BF16)
    empty = jnp.zeros((16, 128), BF16)
    for d in range(16):
        for row in range(3 * SLICE, PACK, 16):
            half, chunk, z_hi, at = spot(d, row)
            packed[half, chunk, z_hi, at : at + 16, :] = band[d] if row == 3 * SLICE else empty

    for p in range(3):
        lhs = xs[1, p * COLS : p * COLS + PIX, :]
        for q in range(3):
            part = dot(lhs, ds[q], TN).astype(BF16)
            put(packed, 0, 3 * p + q, part[:, 0:C2])
            put(packed, 1, 3 * p + q, part[:, C2:C1])

    mine = core[0]
    send_copy = pltpu.make_async_copy(packed.at[1 - mine], send, sems.at[1])
    send_copy.start()
    keep_copy = pltpu.make_async_copy(packed.at[mine], keep, sems.at[0])
    keep_copy.start()
    send_copy.wait()
    keep_copy.wait()


VMEM = pl.BlockSpec(memory_space=pltpu.VMEM)
HBM = pl.BlockSpec(memory_space=pltpu.HBM)
SMEM = pl.BlockSpec(memory_space=pltpu.SMEM)
ANYWHERE = pl.BlockSpec(memory_space=pl.ANY)


def main_work(core, above, below, cot, x, w1, bias, w2):
    parts = (2 * PIECES, 4, PIECE, 128)
    return pl.pallas_call(
        main_body,
        out_shape=(
            jax.ShapeDtypeStruct((PIX, C1), BF16),
            jax.ShapeDtypeStruct((COLS, C1), BF16),
            jax.ShapeDtypeStruct((COLS, C1), BF16),
            jax.ShapeDtypeStruct(parts, BF16),
            jax.ShapeDtypeStruct(parts, BF16),
        ),
        in_specs=[SMEM] + [VMEM] * 3 + [HBM] * 4,
        out_specs=(VMEM, VMEM, VMEM, ANYWHERE, ANYWHERE),
        scratch_shapes=[
            pltpu.VMEM((3, PIX + 2 * COLS, C1), BF16),
            pltpu.VMEM((128 * 10, C2), BF16),
            pltpu.VMEM((PIX, 9 * C2), BF16),
            pltpu.VMEM((3, PIX, C1), BF16),
            pltpu.VMEM((2,) + parts, BF16),
            pltpu.VMEM((PIX, C1), BF16),
            pltpu.VMEM((9, C1, C1), BF16),
            pltpu.VMEM((1, C1), F32),
            pltpu.VMEM((9, C1, C2), BF16),
            pltpu.SemaphoreType.DMA((6,)),
        ],
        compiler_params=pltpu.CompilerParams(vmem_limit_bytes=12 * 2**20),
        cost_estimate=pl.CostEstimate(
            flops=1_100_000_000, bytes_accessed=5_000_000, transcendentals=70_000
        ),
        name="main_work",
    )(core, above, below, cot, x, w1, bias, w2)


def input_body(delta, above, below, w1_hbm, grad_x, ext, ds, w1, sem):
    w1_copy = pltpu.make_async_copy(w1_hbm, w1, sem)
    w1_copy.start()
    ext[0:COLS, :] = above[...]
    ext[COLS : COLS + PIX, :] = delta[...]
    ext[COLS + PIX :, :] = below[...]
    wide = ext[...].astype(F32)
    ds[0] = shifted(wide, 1).astype(BF16)
    ds[1] = ext[...]
    ds[2] = shifted(wide, -1).astype(BF16)
    w1_copy.wait()
    total = jnp.zeros((PIX, C1), F32)
    for p in range(3):
        for q in range(3):
            at = COLS * (2 - p)
            total = total + dot(ds[q, at : at + PIX, :], w1[3 * p + q], NT)
    grad_x[...] = total.astype(BF16)


def input_work(delta, above, below, w1):
    return pl.pallas_call(
        input_body,
        out_shape=jax.ShapeDtypeStruct((PIX, C1), BF16),
        in_specs=[VMEM] * 3 + [HBM],
        out_specs=VMEM,
        scratch_shapes=[
            pltpu.VMEM((PIX + 2 * COLS, C1), BF16),
            pltpu.VMEM((3, PIX + 2 * COLS, C1), BF16),
            pltpu.VMEM((9, C1, C1), BF16),
            pltpu.SemaphoreType.DMA,
        ],
        compiler_params=pltpu.CompilerParams(vmem_limit_bytes=12 * 2**20),
        cost_estimate=pl.CostEstimate(
            flops=300_000_000, bytes_accessed=2_000_000, transcendentals=0
        ),
        name="input_work",
    )(delta, above, below, w1)


def unpack(scale_low, scale_high, full, first, second, bias):
    def rows(start):
        return full[start : start + SLICE, :].astype(F32)

    first[:, 0:C2] = rows(0) * scale_low
    first[:, C2:C1] = rows(SLICE) * scale_low
    second[...] = rows(2 * SLICE) * scale_high
    bias[...] = full[3 * SLICE : 3 * SLICE + 16, :].astype(F32)[0:1, 0:16] * scale_low


def results(full, scale_low, scale_high):
    return pl.pallas_call(
        lambda *refs: unpack(scale_low, scale_high, *refs),
        out_shape=(
            jax.ShapeDtypeStruct((SLICE, C1), F32),
            jax.ShapeDtypeStruct((SLICE, C2), F32),
            jax.ShapeDtypeStruct((1, 16), F32),
        ),
        in_specs=[pl.BlockSpec(memory_space=pltpu.VMEM)],
        out_specs=(pl.BlockSpec(memory_space=pltpu.VMEM),) * 3,
        name="unpack",
    )(full)


FOUR = range(4)
TWO = range(2)


def place(x, z_hi, y, zb, za, core):
    return (x * 4 + z_hi) * 32 + y * 8 + zb * 4 + za * 2 + core


BLOCK = [
    [place(x, zh, y, zb, za, c) for x in FOUR for y in FOUR for za in TWO]
    for zh in FOUR
    for zb in TWO
    for c in TWO
]
COLUMN = [
    [place(x, zh, y, zb, za, c) for zh in FOUR for zb in TWO]
    for x in FOUR
    for y in FOUR
    for za in TWO
    for c in TWO
]
SHARE = [[place(0, 0, y, zb, za, c) for c in TWO for y in FOUR for za in TWO] for zb in TWO]
QUADS = [[4 * j + b for b in FOUR] for j in range(8)]


def added(pieces):
    return jnp.sum(pieces.astype(F32), axis=0).astype(BF16)


def shards(cotangent, inputs, w_first, bias_first, w_second):
    rank = lax.axis_index("rows")
    down = [(i, i + 4) for i in range(28)]
    up = [(i + 4, i) for i in range(28)]
    both = ("dp", "rows")
    x = inputs[0]

    cot = lax.all_to_all(cotangent, "rows", 0, 0, axis_index_groups=QUADS)
    cot = cot.reshape(8, 128, C2)

    def halo(cot_rows, x_row):
        row = jnp.concatenate([x_row[:, :C2], x_row[:, C2:]], axis=0)
        return jnp.concatenate([cot_rows, row[None]])

    above = lax.ppermute(halo(cot[7:8], x[3]), "rows", down)
    below = lax.ppermute(halo(cot[0:1], x[0]), "rows", up)
    core = (rank % 2).astype(jnp.int32).reshape(1)
    x_flat, w1, bias, w2 = (
        pltpu.with_memory_space_constraint(value, pltpu.HBM)
        for value in (
            x.reshape(PIX, C1),
            w_first.reshape(9, C1, C1),
            bias_first.reshape(1, C1),
            w_second.reshape(9, C1, C2),
        )
    )
    cot = cot.reshape(8 * 128, C2)
    delta, delta_first, delta_last, keep, send = main_work(
        core, above, below, cot, x_flat, w1, bias, w2
    )
    received = lax.ppermute(send, "rows", [(i, i ^ 1) for i in range(32)])
    from_above = lax.ppermute(delta_last, "rows", down)
    from_below = lax.ppermute(delta_first, "rows", up)

    pair = (keep.astype(F32) + received.astype(F32)).astype(BF16)
    block = lax.all_to_all(pair, both, 0, 0, axis_index_groups=BLOCK)
    block, from_above, from_below = lax.optimization_barrier((block, from_above, from_below))
    block = added(block)
    grad_x = input_work(delta, from_above, from_below, w1)
    spread = jnp.broadcast_to(block[:, None], (4, 2, PIECE, 128)).reshape(8, PIECE, 128)
    column = lax.all_to_all(spread, both, 0, 0, axis_index_groups=COLUMN)
    column, grad_x = lax.optimization_barrier((column, grad_x))
    piece = added(column)
    copies = jnp.broadcast_to(piece[None], (PIECES, PIECE, 128))
    full = lax.all_to_all(copies, "rows", 0, 0, axis_index_groups=SHARE)

    pixels_low = lax.axis_size("dp") * lax.axis_size("rows") * PIX
    scale_low = pixels_low ** (-0.5)
    scale_high = (4 * pixels_low) ** (-0.5)
    grad_first, grad_second, grad_bias = results(full.reshape(PACK, 128), scale_low, scale_high)
    grad_input = grad_x.reshape(1, ROWS, COLS, C1)
    return grad_input, grad_first, grad_second, grad_bias.reshape(16)


def solution(mesh):
    in_specs = (P("dp", "rows", None, None), P("dp", "rows", None, None), P(), P(), P())
    out_specs = (P("dp", "rows", None, None), P("dp", None), P("dp", None), P("dp"))
    return jax.shard_map(shards, mesh=mesh, in_specs=in_specs, out_specs=out_specs, check_vma=False)
```

```python
import jax
import jax.numpy as jnp
from jax import lax
from jax.experimental import pallas as pl
from jax.experimental.pallas import tpu as pltpu
from jax.sharding import PartitionSpec as P

F32 = jnp.float32
BF16 = jnp.bfloat16
COLS = 64
C1 = 256
C2 = 128
ROWS = 4
PIX = ROWS * COLS
SLICE = 144
PIECE = 32
PIECES = 16
PACK = PIECE * PIECES


def dot(a, b, contract):
    return lax.dot_general(a, b, (contract, ((), ())), preferred_element_type=F32)


NN = ((1,), (0,))
NT = ((1,), (1,))
TN = ((0,), (0,))


def shifted(value, by):
    length = value.shape[0]
    column = lax.broadcasted_iota(jnp.int32, value.shape, 0) % COLS
    rolled = pltpu.roll(value, (-by) % length, 0)
    inside = (column + by >= 0) & (column + by < COLS)
    return jnp.where(inside, rolled, 0.0)


def spot(d, row):
    piece, inner = divmod(row, PIECE)
    half, rest = divmod(piece, PIECES // 2)
    x, z_hi = divmod(d, 4)
    return half, x * (PIECES // 2) + rest, z_hi, inner


def put(packed, band, tap, value):
    row = 0
    while row < C1:
        d, inner = divmod(tap * C1 + row, SLICE)
        half, chunk, z_hi, at = spot(d, band * SLICE + inner)
        count = min(C1 - row, SLICE - inner, PIECE - at)
        packed[half, chunk, z_hi, at : at + count, :] = value[row : row + count, :]
        row += count


def pick_columns():
    out_row = lax.broadcasted_iota(jnp.int32, (3 * COLS, 256), 0)
    column = lax.broadcasted_iota(jnp.int32, (3 * COLS, 256), 1) % 128
    left = 2 * (out_row % COLS) + 1 - out_row // COLS
    return ((column == left) | (column == left + 1)).astype(F32).astype(BF16)


def silu_parts(preact):
    sigma = 1.0 / (1.0 + jnp.exp(-preact))
    return preact * sigma, sigma * (1.0 + preact * (1.0 - sigma))


def start(source, target, sem):
    copy = pltpu.make_async_copy(source, target, sem)
    copy.start()
    return copy


def conv_body(x_hbm, w1_hbm, bias_hbm, preact, w1_edge, xs, x, w1, bias, sems):
    x_copy = start(x_hbm, x, sems.at[0])
    bias_copy = start(bias_hbm, bias, sems.at[1])
    w1_copy = start(w1_hbm, w1, sems.at[2])
    x_copy.wait()
    wide = x[...].astype(F32)
    xs[0] = shifted(wide, -1).astype(BF16)
    xs[1] = x[...]
    xs[2] = shifted(wide, 1).astype(BF16)
    bias_copy.wait()
    w1_copy.wait()
    same = jnp.broadcast_to(bias[...], (PIX, C1))
    lower = jnp.zeros((PIX - COLS, C1), F32)
    upper = jnp.zeros((PIX - COLS, C1), F32)
    for q in range(3):
        lower = lower + dot(xs[q, 0 : PIX - COLS, :], w1[q], NN)
        same = same + dot(xs[q], w1[3 + q], NN)
        upper = upper + dot(xs[q, COLS:PIX, :], w1[6 + q], NN)
    preact[0:COLS, :] = same[0:COLS] + upper[0:COLS]
    middle = slice(COLS, PIX - COLS)
    preact[middle, :] = same[middle] + upper[COLS:] + lower[: PIX - 2 * COLS]
    preact[PIX - COLS :, :] = same[PIX - COLS :] + lower[PIX - 2 * COLS :]
    w1_edge[0:3] = w1[0:3]
    w1_edge[3:6] = w1[6:9]


def boxes_body(cot, w2_hbm, boxes, grad_act, w2_edge, w2, sem):
    w2_copy = start(w2_hbm, w2, sem)
    pick = pick_columns()
    zero = jnp.zeros((COLS, 3 * C2), BF16)
    boxes[0:COLS, 6 * C2 :] = zero
    boxes[PIX - COLS :, 0 : 3 * C2] = zero
    for h in range(7):
        sums = dot(pick, cot[128 * h : 128 * (h + 2), :], NN).astype(BF16)
        for p in range(3):
            if (h + p - 1) % 2 == 0 and 0 <= (h + p - 1) // 2 < ROWS:
                i = (h + p - 1) // 2
                for q in range(3):
                    t = 3 * p + q
                    boxes[COLS * i : COLS * (i + 1), C2 * t : C2 * (t + 1)] = sums[
                        COLS * q : COLS * (q + 1), :
                    ]
    w2_copy.wait()
    total = jnp.zeros((PIX, C1), F32)
    for t in range(9):
        total = total + dot(boxes[:, C2 * t : C2 * (t + 1)], w2[t], NT)
    grad_act[...] = total
    w2_edge[0:3] = w2[6:9]
    w2_edge[3:6] = w2[0:3]


def main_body(
    core, above, below, cot, preact_in, boxes_in, grad_act_in, w1_edge, w2_edge, x_hbm,
    delta_out, delta_first, delta_last, packed, send,
    x, boxes, ds, preact, grad_act, sems,
):
    x_copy = start(x_hbm, x.at[COLS : COLS + PIX], sems.at[4])

    boxes[...] = boxes_in[...]
    grad_act[...] = grad_act_in[...]
    preact[...] = preact_in[...]
    pick = pick_columns()
    first, last = slice(0, COLS), slice(PIX - COLS, PIX)
    for rows, p, pair in (
        (first, 2, (above[0], cot[0:128, :])),
        (last, 0, (cot[128 * 7 : 128 * 8, :], below[0])),
    ):
        sums = dot(pick, jnp.concatenate(pair), NN).astype(BF16)
        for q in range(3):
            t = 3 * p + q
            boxes[rows, C2 * t : C2 * (t + 1)] = sums[COLS * q : COLS * (q + 1), :]
    for at, halo in ((0, above), (COLS + PIX, below)):
        x[at : at + COLS, 0:C2] = halo[1, 0:COLS, :]
        x[at : at + COLS, C2:C1] = halo[1, COLS : 2 * COLS, :]
    for side, rows, p in ((0, first, 2), (1, last, 0)):
        part = grad_act[rows, :]
        for q in range(3):
            t = 3 * p + q
            part = part + dot(boxes[rows, C2 * t : C2 * (t + 1)], w2_edge[3 * side + q], NT)
        grad_act[rows, :] = part
    for side, rows, at in ((0, first, 0), (1, last, COLS + PIX)):
        wide = x[at : at + COLS, :].astype(F32)
        part = preact[rows, :]
        for q in range(3):
            part = part + dot(shifted(wide, q - 1).astype(BF16), w1_edge[3 * side + q], NN)
        preact[rows, :] = part
    act, slope = silu_parts(preact[...])
    second = dot(act.astype(BF16), boxes[...], TN).astype(BF16)
    for t in range(9):
        put(packed, 2, t, second[:, C2 * t : C2 * (t + 1)])

    delta = (grad_act[...] * slope).astype(BF16)
    delta_out[...] = delta
    delta_first[...] = delta[0:COLS]
    delta_last[...] = delta[PIX - COLS : PIX]
    wide = delta.astype(F32)
    ds[0] = shifted(wide, 1).astype(BF16)
    ds[1] = delta
    ds[2] = shifted(wide, -1).astype(BF16)

    total = jnp.sum(wide, axis=0, keepdims=True).astype(BF16).astype(F32)
    owner = lax.broadcasted_iota(jnp.int32, (16, C1), 0)
    channel = lax.broadcasted_iota(jnp.int32, (16, C1), 1)
    spread = jnp.where(channel // 16 == owner, jnp.broadcast_to(total, (16, C1)), 0.0)
    source = lax.broadcasted_iota(jnp.int32, (C1, 128), 0)
    lane = lax.broadcasted_iota(jnp.int32, (C1, 128), 1)
    fold = (source % 16 == lane).astype(F32).astype(BF16)
    folded = dot(spread.astype(BF16), fold, NN)
    row = lax.broadcasted_iota(jnp.int32, (16, 16, 128), 1)
    band = jnp.where(row == 0, jnp.broadcast_to(folded[:, None, :], (16, 16, 128)), 0.0)
    band = band.astype(BF16)
    empty = jnp.zeros((16, 128), BF16)
    for d in range(16):
        for row in range(3 * SLICE, PACK, 16):
            half, chunk, z_hi, at = spot(d, row)
            packed[half, chunk, z_hi, at : at + 16, :] = band[d] if row == 3 * SLICE else empty

    mine = core[0]
    copies = []
    x_copy.wait()
    for p in range(3):
        lhs = x[p * COLS : p * COLS + PIX, :]
        for q in range(3):
            tap = 3 * p + q
            part = dot(lhs, ds[q], TN).astype(BF16)
            put(packed, 0, tap, part[:, 0:C2])
            put(packed, 1, tap, part[:, C2:C1])
            if tap in (2, 4, 6, 8):
                n = tap // 2 - 1
                chunks = pl.ds(n * (PIECES // 2), PIECES // 2)
                copies.append(start(packed.at[1 - mine, chunks], send.at[chunks], sems.at[n]))
    for copy in copies:
        copy.wait()


VMEM = pl.BlockSpec(memory_space=pltpu.VMEM)
HBM = pl.BlockSpec(memory_space=pltpu.HBM)
SMEM = pl.BlockSpec(memory_space=pltpu.SMEM)
ANYWHERE = pl.BlockSpec(memory_space=pl.ANY)


def conv_work(x, w1, bias):
    return pl.pallas_call(
        conv_body,
        out_shape=(
            jax.ShapeDtypeStruct((PIX, C1), F32),
            jax.ShapeDtypeStruct((6, C1, C1), BF16),
        ),
        in_specs=[HBM] * 3,
        out_specs=(VMEM, VMEM),
        scratch_shapes=[
            pltpu.VMEM((3, PIX, C1), BF16),
            pltpu.VMEM((PIX, C1), BF16),
            pltpu.VMEM((9, C1, C1), BF16),
            pltpu.VMEM((1, C1), F32),
            pltpu.SemaphoreType.DMA((3,)),
        ],
        compiler_params=pltpu.CompilerParams(vmem_limit_bytes=12 * 2**20),
        cost_estimate=pl.CostEstimate(
            flops=300_000_000, bytes_accessed=1_500_000, transcendentals=0
        ),
        name="conv_work",
    )(x, w1, bias)


def boxes_work(cot, w2):
    return pl.pallas_call(
        boxes_body,
        out_shape=(
            jax.ShapeDtypeStruct((PIX, 9 * C2), BF16),
            jax.ShapeDtypeStruct((PIX, C1), F32),
            jax.ShapeDtypeStruct((6, C1, C2), BF16),
        ),
        in_specs=[VMEM, HBM],
        out_specs=(VMEM, VMEM, VMEM),
        scratch_shapes=[pltpu.VMEM((9, C1, C2), BF16), pltpu.SemaphoreType.DMA],
        compiler_params=pltpu.CompilerParams(vmem_limit_bytes=12 * 2**20),
        cost_estimate=pl.CostEstimate(
            flops=300_000_000, bytes_accessed=1_500_000, transcendentals=0
        ),
        name="boxes_work",
    )(cot, w2)


PARTS = (2 * PIECES, 4, PIECE, 128)


def main_work(core, above, below, cot, preact, boxes, grad_act, w1_edge, w2_edge, x):
    return pl.pallas_call(
        main_body,
        out_shape=(
            jax.ShapeDtypeStruct((PIX, C1), BF16),
            jax.ShapeDtypeStruct((COLS, C1), BF16),
            jax.ShapeDtypeStruct((COLS, C1), BF16),
            jax.ShapeDtypeStruct((2,) + PARTS, BF16),
            jax.ShapeDtypeStruct(PARTS, BF16),
        ),
        in_specs=[SMEM] + [VMEM] * 8 + [HBM],
        out_specs=(VMEM, VMEM, VMEM, VMEM, ANYWHERE),
        scratch_shapes=[
            pltpu.VMEM((PIX + 2 * COLS, C1), BF16),
            pltpu.VMEM((PIX, 9 * C2), BF16),
            pltpu.VMEM((3, PIX, C1), BF16),
            pltpu.VMEM((PIX, C1), F32),
            pltpu.VMEM((PIX, C1), F32),
            pltpu.SemaphoreType.DMA((5,)),
        ],
        compiler_params=pltpu.CompilerParams(vmem_limit_bytes=16 * 2**20),
        cost_estimate=pl.CostEstimate(
            flops=600_000_000, bytes_accessed=5_000_000, transcendentals=70_000
        ),
        name="main_work",
    )(core, above, below, cot, preact, boxes, grad_act, w1_edge, w2_edge, x)


def pair_body(core, packed, received, pair, total, sems):
    mine = core[0]
    copies = []
    for n in range(4):
        chunks = pl.ds(n * (PIECES // 2), PIECES // 2)
        total[chunks] = packed[mine, chunks] + received[chunks]
        copies.append(start(total.at[chunks], pair.at[chunks], sems.at[n]))
    for copy in copies:
        copy.wait()


def pair_work(core, packed, received):
    return pl.pallas_call(
        pair_body,
        out_shape=jax.ShapeDtypeStruct(PARTS, BF16),
        in_specs=[SMEM, VMEM, VMEM],
        out_specs=ANYWHERE,
        scratch_shapes=[pltpu.VMEM(PARTS, BF16), pltpu.SemaphoreType.DMA((4,))],
        compiler_params=pltpu.CompilerParams(vmem_limit_bytes=8 * 2**20),
        name="pair_work",
    )(core, packed, received)


def sum_body(copies, pieces, out):
    total = pieces[0].astype(F32)
    for n in range(1, pieces.shape[0]):
        total = total + pieces[n].astype(F32)
    for n in range(copies):
        out[n] = total.astype(BF16)


def sum_work(pieces, copies):
    return pl.pallas_call(
        lambda *refs: sum_body(copies, *refs),
        out_shape=jax.ShapeDtypeStruct((copies,) + pieces.shape[1:], BF16),
        in_specs=[VMEM],
        out_specs=VMEM,
        compiler_params=pltpu.CompilerParams(vmem_limit_bytes=4 * 2**20),
        name="sum_work",
    )(pieces)


def input_body(delta, above, below, w1_hbm, grad_x, ext, ds, w1, sem):
    w1_copy = pltpu.make_async_copy(w1_hbm, w1, sem)
    w1_copy.start()
    ext[0:COLS, :] = above[...]
    ext[COLS : COLS + PIX, :] = delta[...]
    ext[COLS + PIX :, :] = below[...]
    wide = ext[...].astype(F32)
    ds[0] = shifted(wide, 1).astype(BF16)
    ds[1] = ext[...]
    ds[2] = shifted(wide, -1).astype(BF16)
    w1_copy.wait()
    total = jnp.zeros((PIX, C1), F32)
    for p in range(3):
        for q in range(3):
            at = COLS * (2 - p)
            total = total + dot(ds[q, at : at + PIX, :], w1[3 * p + q], NT)
    grad_x[...] = total.astype(BF16)


def input_work(delta, above, below, w1):
    return pl.pallas_call(
        input_body,
        out_shape=jax.ShapeDtypeStruct((PIX, C1), BF16),
        in_specs=[VMEM] * 3 + [HBM],
        out_specs=VMEM,
        scratch_shapes=[
            pltpu.VMEM((PIX + 2 * COLS, C1), BF16),
            pltpu.VMEM((3, PIX + 2 * COLS, C1), BF16),
            pltpu.VMEM((9, C1, C1), BF16),
            pltpu.SemaphoreType.DMA,
        ],
        compiler_params=pltpu.CompilerParams(vmem_limit_bytes=12 * 2**20),
        cost_estimate=pl.CostEstimate(
            flops=300_000_000, bytes_accessed=2_000_000, transcendentals=0
        ),
        name="input_work",
    )(delta, above, below, w1)


def unpack(scale_low, scale_high, full, first, second, bias):
    def rows(start):
        return full[start : start + SLICE, :].astype(F32)

    first[:, 0:C2] = rows(0) * scale_low
    first[:, C2:C1] = rows(SLICE) * scale_low
    second[...] = rows(2 * SLICE) * scale_high
    bias[...] = full[3 * SLICE : 3 * SLICE + 16, :].astype(F32)[0:1, 0:16] * scale_low


def results(full, scale_low, scale_high):
    return pl.pallas_call(
        lambda *refs: unpack(scale_low, scale_high, *refs),
        out_shape=(
            jax.ShapeDtypeStruct((SLICE, C1), F32),
            jax.ShapeDtypeStruct((SLICE, C2), F32),
            jax.ShapeDtypeStruct((1, 16), F32),
        ),
        in_specs=[pl.BlockSpec(memory_space=pltpu.VMEM)],
        out_specs=(pl.BlockSpec(memory_space=pltpu.VMEM),) * 3,
        name="unpack",
    )(full)


FOUR = range(4)
TWO = range(2)


def place(x, z_hi, y, zb, za, core):
    return (x * 4 + z_hi) * 32 + y * 8 + zb * 4 + za * 2 + core


BLOCK = [
    [place(x, zh, y, zb, za, c) for x in FOUR for y in FOUR for za in TWO]
    for zh in FOUR
    for zb in TWO
    for c in TWO
]
COLUMN = [
    [place(x, zh, y, zb, za, c) for zb in TWO for zh in FOUR]
    for x in FOUR
    for y in FOUR
    for za in TWO
    for c in TWO
]
SHARE = [[place(0, 0, y, zb, za, c) for c in TWO for y in FOUR for za in TWO] for zb in TWO]
QUADS = [[4 * j + b for b in FOUR] for j in range(8)]


def shards(cotangent, inputs, w_first, bias_first, w_second):
    rank = lax.axis_index("rows")
    down = [(i, i + 4) for i in range(28)]
    up = [(i + 4, i) for i in range(28)]
    both = ("dp", "rows")
    x = inputs[0]

    cot = lax.all_to_all(cotangent, "rows", 0, 0, axis_index_groups=QUADS)
    cot = cot.reshape(8, 128, C2)

    def halo(cot_rows, x_row):
        row = jnp.concatenate([x_row[:, :C2], x_row[:, C2:]], axis=0)
        return jnp.concatenate([cot_rows, row[None]])

    above = lax.ppermute(halo(cot[7:8], x[3]), "rows", down)
    below = lax.ppermute(halo(cot[0:1], x[0]), "rows", up)
    core = (rank % 2).astype(jnp.int32).reshape(1)
    x_flat, w1, bias, w2 = (
        pltpu.with_memory_space_constraint(value, pltpu.HBM)
        for value in (
            x.reshape(PIX, C1),
            w_first.reshape(9, C1, C1),
            bias_first.reshape(1, C1),
            w_second.reshape(9, C1, C2),
        )
    )
    cot = cot.reshape(8 * 128, C2)
    preact, w1_edge = conv_work(x_flat, w1, bias)
    boxes, grad_act, w2_edge = boxes_work(cot, w2)
    delta, delta_first, delta_last, packed, send = main_work(
        core, above, below, cot, preact, boxes, grad_act, w1_edge, w2_edge, x_flat
    )
    received = lax.ppermute(send, "rows", [(i, i ^ 1) for i in range(32)])
    from_above = lax.ppermute(delta_last, "rows", down)
    from_below = lax.ppermute(delta_first, "rows", up)

    pair = pair_work(core, packed, received)
    block = lax.all_to_all(pair, both, 0, 0, axis_index_groups=BLOCK)
    block, from_above, from_below = lax.optimization_barrier((block, from_above, from_below))
    grad_x = input_work(delta, from_above, from_below, w1)
    spread = sum_work(block, 2).reshape(8, PIECE, 128)
    column = lax.all_to_all(spread, both, 0, 0, axis_index_groups=COLUMN)
    column, grad_x = lax.optimization_barrier((column, grad_x))
    full = lax.all_to_all(sum_work(column, PIECES), "rows", 0, 0, axis_index_groups=SHARE)

    pixels_low = lax.axis_size("dp") * lax.axis_size("rows") * PIX
    scale_low = pixels_low ** (-0.5)
    scale_high = (4 * pixels_low) ** (-0.5)
    full = pltpu.with_memory_space_constraint(full.reshape(PACK, 128), pltpu.VMEM)
    grad_first, grad_second, grad_bias = results(full, scale_low, scale_high)
    grad_input = grad_x.reshape(1, ROWS, COLS, C1)
    return grad_input, grad_first, grad_second, grad_bias.reshape(16)


def solution(mesh):
    in_specs = (P("dp", "rows", None, None), P("dp", "rows", None, None), P(), P(), P())
    out_specs = (P("dp", "rows", None, None), P("dp", None), P("dp", None), P("dp"))
    return jax.shard_map(shards, mesh=mesh, in_specs=in_specs, out_specs=out_specs, check_vma=False)
```

```python
import jax
import jax.numpy as jnp
from jax import lax
from jax.experimental import pallas as pl
from jax.experimental.pallas import tpu as pltpu
from jax.sharding import PartitionSpec as P

F32 = jnp.float32
BF16 = jnp.bfloat16
COLS = 64
C1 = 256
C2 = 128
ROWS = 4
PIX = ROWS * COLS
SLICE = 144
TILES = 28
PIECE = (32, 128)
PIECES = 16
CHUNK = 16 * TILES // 4
PARTS = (CHUNK, 32, 128)


def dot(a, b, contract):
    return lax.dot_general(a, b, (contract, ((), ())), preferred_element_type=F32)


NN = ((1,), (0,))
NT = ((1,), (1,))
TN = ((0,), (0,))


def shifted(value, by):
    length = value.shape[0]
    column = lax.broadcasted_iota(jnp.int32, value.shape, 0) % COLS
    rolled = pltpu.roll(value, (-by) % length, 0)
    inside = (column + by >= 0) & (column + by < COLS)
    return jnp.where(inside, rolled, 0.0)


def tiles_of(k, z_hi):
    return 1 if k % 4 == z_hi else 2


def spot(d, tile):
    half, tile = divmod(tile, TILES // 2)
    x, z_hi = divmod(d, 4)
    k = 0
    while tile >= tiles_of(k, z_hi):
        tile -= tiles_of(k, z_hi)
        k += 1
    before = sum(tiles_of(k, z) for z in range(z_hi)) + tile
    return half, CHUNK * (x * 8 + k) + 16 * before


def put(packed, band, tap, value):
    for row in range(0, C1, 16):
        d, inner = divmod(tap * C1 + row, SLICE)
        half, at = spot(d, band * (SLICE // 16) + inner // 16)
        packed[half, at // 32, at % 32 : at % 32 + 16, :] = value[row : row + 16, :]


def pick_columns():
    out_row = lax.broadcasted_iota(jnp.int32, (3 * COLS, 256), 0)
    column = lax.broadcasted_iota(jnp.int32, (3 * COLS, 256), 1) % 128
    left = 2 * (out_row % COLS) + 1 - out_row // COLS
    return ((column == left) | (column == left + 1)).astype(F32).astype(BF16)


def silu_parts(preact):
    sigma = 1.0 / (1.0 + jnp.exp(-preact))
    return preact * sigma, sigma * (1.0 + preact * (1.0 - sigma))


def start(source, target, sem):
    copy = pltpu.make_async_copy(source, target, sem)
    copy.start()
    return copy


def conv_body(x_hbm, w1_hbm, bias_hbm, preact, w1_edge, xs, x, w1, bias, sems):
    x_copy = start(x_hbm, x, sems.at[0])
    bias_copy = start(bias_hbm, bias, sems.at[1])
    w1_copy = start(w1_hbm, w1, sems.at[2])
    x_copy.wait()
    wide = x[...].astype(F32)
    xs[0] = shifted(wide, -1).astype(BF16)
    xs[1] = x[...]
    xs[2] = shifted(wide, 1).astype(BF16)
    bias_copy.wait()
    w1_copy.wait()
    same = jnp.broadcast_to(bias[...], (PIX, C1))
    lower = jnp.zeros((PIX - COLS, C1), F32)
    upper = jnp.zeros((PIX - COLS, C1), F32)
    for q in range(3):
        lower = lower + dot(xs[q, 0 : PIX - COLS, :], w1[q], NN)
        same = same + dot(xs[q], w1[3 + q], NN)
        upper = upper + dot(xs[q, COLS:PIX, :], w1[6 + q], NN)
    preact[0:COLS, :] = same[0:COLS] + upper[0:COLS]
    middle = slice(COLS, PIX - COLS)
    preact[middle, :] = same[middle] + upper[COLS:] + lower[: PIX - 2 * COLS]
    preact[PIX - COLS :, :] = same[PIX - COLS :] + lower[PIX - 2 * COLS :]
    w1_edge[0:3] = w1[0:3]
    w1_edge[3:6] = w1[6:9]


def boxes_body(cot, w2_hbm, boxes, grad_act, w2_edge, w2, sem):
    w2_copy = start(w2_hbm, w2, sem)
    pick = pick_columns()
    zero = jnp.zeros((COLS, 3 * C2), BF16)
    boxes[0:COLS, 6 * C2 :] = zero
    boxes[PIX - COLS :, 0 : 3 * C2] = zero
    for h in range(7):
        sums = dot(pick, cot[128 * h : 128 * (h + 2), :], NN).astype(BF16)
        for p in range(3):
            if (h + p - 1) % 2 == 0 and 0 <= (h + p - 1) // 2 < ROWS:
                i = (h + p - 1) // 2
                for q in range(3):
                    t = 3 * p + q
                    boxes[COLS * i : COLS * (i + 1), C2 * t : C2 * (t + 1)] = sums[
                        COLS * q : COLS * (q + 1), :
                    ]
    w2_copy.wait()
    total = jnp.zeros((PIX, C1), F32)
    for t in range(9):
        total = total + dot(boxes[:, C2 * t : C2 * (t + 1)], w2[t], NT)
    grad_act[...] = total
    w2_edge[0:3] = w2[6:9]
    w2_edge[3:6] = w2[0:3]


def main_body(
    code, above, below, cot, preact_in, boxes_in, grad_act_in, w1_edge, w2_edge, x_hbm,
    delta_out, delta_first, delta_last, packed, send,
    x, boxes, ds, preact, grad_act, sems,
):
    x_copy = start(x_hbm, x.at[COLS : COLS + PIX], sems.at[1])

    boxes[...] = boxes_in[...]
    grad_act[...] = grad_act_in[...]
    preact[...] = preact_in[...]
    pick = pick_columns()
    first, last = slice(0, COLS), slice(PIX - COLS, PIX)
    for rows, p, pair in (
        (first, 2, (above[0], cot[0:128, :])),
        (last, 0, (cot[128 * 7 : 128 * 8, :], below[0])),
    ):
        sums = dot(pick, jnp.concatenate(pair), NN).astype(BF16)
        for q in range(3):
            t = 3 * p + q
            boxes[rows, C2 * t : C2 * (t + 1)] = sums[COLS * q : COLS * (q + 1), :]
    for at, halo in ((0, above), (COLS + PIX, below)):
        x[at : at + COLS, 0:C2] = halo[1, 0:COLS, :]
        x[at : at + COLS, C2:C1] = halo[1, COLS : 2 * COLS, :]
    for side, rows, p in ((0, first, 2), (1, last, 0)):
        part = grad_act[rows, :]
        for q in range(3):
            t = 3 * p + q
            part = part + dot(boxes[rows, C2 * t : C2 * (t + 1)], w2_edge[3 * side + q], NT)
        grad_act[rows, :] = part
    for side, rows, at in ((0, first, 0), (1, last, COLS + PIX)):
        wide = x[at : at + COLS, :].astype(F32)
        part = preact[rows, :]
        for q in range(3):
            part = part + dot(shifted(wide, q - 1).astype(BF16), w1_edge[3 * side + q], NN)
        preact[rows, :] = part
    act, slope = silu_parts(preact[...])
    second = dot(act.astype(BF16), boxes[...], TN).astype(BF16)
    for t in range(9):
        put(packed, 2, t, second[:, C2 * t : C2 * (t + 1)])

    delta = (grad_act[...] * slope).astype(BF16)
    delta_out[...] = delta
    delta_first[...] = delta[0:COLS]
    delta_last[...] = delta[PIX - COLS : PIX]
    wide = delta.astype(F32)
    ds[0] = shifted(wide, 1).astype(BF16)
    ds[1] = delta
    ds[2] = shifted(wide, -1).astype(BF16)

    total = jnp.sum(wide, axis=0, keepdims=True).astype(BF16).astype(F32)
    owner = lax.broadcasted_iota(jnp.int32, (16, C1), 0)
    channel = lax.broadcasted_iota(jnp.int32, (16, C1), 1)
    spread = jnp.where(channel // 16 == owner, jnp.broadcast_to(total, (16, C1)), 0.0)
    source = lax.broadcasted_iota(jnp.int32, (C1, 128), 0)
    lane = lax.broadcasted_iota(jnp.int32, (C1, 128), 1)
    fold = (source % 16 == lane).astype(F32).astype(BF16)
    folded = dot(spread.astype(BF16), fold, NN)
    row = lax.broadcasted_iota(jnp.int32, (16, 16, 128), 1)
    band = jnp.where(row == 0, jnp.broadcast_to(folded[:, None, :], (16, 16, 128)), 0.0)
    band = band.astype(BF16)
    for d in range(16):
        half, at = spot(d, TILES - 1)
        packed[half, at // 32, at % 32 : at % 32 + 16, :] = band[d]

    x_copy.wait()
    for p in range(3):
        lhs = x[p * COLS : p * COLS + PIX, :]
        for q in range(3):
            tap = 3 * p + q
            part = dot(lhs, ds[q], TN).astype(BF16)
            put(packed, 0, tap, part[:, 0:C2])
            put(packed, 1, tap, part[:, C2:C1])
    start(packed.at[1 - code[0] % 2], send, sems.at[0]).wait()


VMEM = pl.BlockSpec(memory_space=pltpu.VMEM)
HBM = pl.BlockSpec(memory_space=pltpu.HBM)
SMEM = pl.BlockSpec(memory_space=pltpu.SMEM)
ANYWHERE = pl.BlockSpec(memory_space=pl.ANY)


def conv_work(x, w1, bias):
    return pl.pallas_call(
        conv_body,
        out_shape=(
            jax.ShapeDtypeStruct((PIX, C1), F32),
            jax.ShapeDtypeStruct((6, C1, C1), BF16),
        ),
        in_specs=[HBM] * 3,
        out_specs=(VMEM, VMEM),
        scratch_shapes=[
            pltpu.VMEM((3, PIX, C1), BF16),
            pltpu.VMEM((PIX, C1), BF16),
            pltpu.VMEM((9, C1, C1), BF16),
            pltpu.VMEM((1, C1), F32),
            pltpu.SemaphoreType.DMA((3,)),
        ],
        compiler_params=pltpu.CompilerParams(vmem_limit_bytes=12 * 2**20),
        cost_estimate=pl.CostEstimate(
            flops=300_000_000, bytes_accessed=1_500_000, transcendentals=0
        ),
        name="conv_work",
    )(x, w1, bias)


def boxes_work(cot, w2):
    return pl.pallas_call(
        boxes_body,
        out_shape=(
            jax.ShapeDtypeStruct((PIX, 9 * C2), BF16),
            jax.ShapeDtypeStruct((PIX, C1), F32),
            jax.ShapeDtypeStruct((6, C1, C2), BF16),
        ),
        in_specs=[VMEM, HBM],
        out_specs=(VMEM, VMEM, VMEM),
        scratch_shapes=[pltpu.VMEM((9, C1, C2), BF16), pltpu.SemaphoreType.DMA],
        compiler_params=pltpu.CompilerParams(vmem_limit_bytes=12 * 2**20),
        cost_estimate=pl.CostEstimate(
            flops=300_000_000, bytes_accessed=1_500_000, transcendentals=0
        ),
        name="boxes_work",
    )(cot, w2)


def main_work(code, above, below, cot, preact, boxes, grad_act, w1_edge, w2_edge, x):
    return pl.pallas_call(
        main_body,
        out_shape=(
            jax.ShapeDtypeStruct((PIX, C1), BF16),
            jax.ShapeDtypeStruct((COLS, C1), BF16),
            jax.ShapeDtypeStruct((COLS, C1), BF16),
            jax.ShapeDtypeStruct((2,) + PARTS, BF16),
            jax.ShapeDtypeStruct(PARTS, BF16),
        ),
        in_specs=[SMEM] + [VMEM] * 8 + [HBM],
        out_specs=(VMEM, VMEM, VMEM, VMEM, ANYWHERE),
        scratch_shapes=[
            pltpu.VMEM((PIX + 2 * COLS, C1), BF16),
            pltpu.VMEM((PIX, 9 * C2), BF16),
            pltpu.VMEM((3, PIX, C1), BF16),
            pltpu.VMEM((PIX, C1), F32),
            pltpu.VMEM((PIX, C1), F32),
            pltpu.SemaphoreType.DMA((2,)),
        ],
        compiler_params=pltpu.CompilerParams(vmem_limit_bytes=16 * 2**20),
        cost_estimate=pl.CostEstimate(
            flops=600_000_000, bytes_accessed=5_000_000, transcendentals=70_000
        ),
        name="main_work",
    )(code, above, below, cot, preact, boxes, grad_act, w1_edge, w2_edge, x)


def pair_body(code, packed, received, pair, total, sems):
    mine = code[0] % 2
    copies = []
    for n in range(4):
        chunks = pl.ds(n * (CHUNK // 4), CHUNK // 4)
        total[chunks] = packed[mine, chunks] + received[chunks]
        copies.append(start(total.at[chunks], pair.at[chunks], sems.at[n]))
    for copy in copies:
        copy.wait()


def pair_work(code, packed, received):
    return pl.pallas_call(
        pair_body,
        out_shape=jax.ShapeDtypeStruct(PARTS, BF16),
        in_specs=[SMEM, VMEM, VMEM],
        out_specs=ANYWHERE,
        scratch_shapes=[pltpu.VMEM(PARTS, BF16), pltpu.SemaphoreType.DMA((4,))],
        compiler_params=pltpu.CompilerParams(vmem_limit_bytes=8 * 2**20),
        name="pair_work",
    )(code, packed, received)


def block_body(code, pieces, out, total):
    value = pieces[0].astype(F32)
    for n in range(1, 32):
        value = value + pieces[n].astype(F32)
    tiles = CHUNK // 16
    total[0:tiles] = value.reshape(tiles, 16, 128)
    total[tiles] = jnp.zeros((16, 128), F32)
    single = code[0] // 2 % 4
    for z_hi in range(4):
        part = total[pl.ds(2 * z_hi - jnp.where(z_hi > single, 1, 0), 2)]
        for n in range(2):
            out[n, z_hi] = part.reshape(PIECE).astype(BF16)


def block_work(code, pieces):
    return pl.pallas_call(
        block_body,
        out_shape=jax.ShapeDtypeStruct((2, 4) + PIECE, BF16),
        in_specs=[SMEM, VMEM],
        out_specs=VMEM,
        scratch_shapes=[pltpu.VMEM((TILES // 4 + 1, 16, 128), F32)],
        compiler_params=pltpu.CompilerParams(vmem_limit_bytes=4 * 2**20),
        name="block_work",
    )(code, pieces)


def column_body(pieces, out):
    total = pieces[0].astype(F32)
    for n in range(1, pieces.shape[0]):
        total = total + pieces[n].astype(F32)
    for n in range(PIECES):
        out[n] = total.astype(BF16)


def column_work(pieces):
    return pl.pallas_call(
        column_body,
        out_shape=jax.ShapeDtypeStruct((PIECES,) + PIECE, BF16),
        in_specs=[VMEM],
        out_specs=VMEM,
        compiler_params=pltpu.CompilerParams(vmem_limit_bytes=4 * 2**20),
        name="column_work",
    )(pieces)


def input_body(delta, above, below, w1_hbm, grad_x, ext, ds, w1, sem):
    w1_copy = pltpu.make_async_copy(w1_hbm, w1, sem)
    w1_copy.start()
    ext[0:COLS, :] = above[...]
    ext[COLS : COLS + PIX, :] = delta[...]
    ext[COLS + PIX :, :] = below[...]
    wide = ext[...].astype(F32)
    ds[0] = shifted(wide, 1).astype(BF16)
    ds[1] = ext[...]
    ds[2] = shifted(wide, -1).astype(BF16)
    w1_copy.wait()
    total = jnp.zeros((PIX, C1), F32)
    for p in range(3):
        for q in range(3):
            at = COLS * (2 - p)
            total = total + dot(ds[q, at : at + PIX, :], w1[3 * p + q], NT)
    grad_x[...] = total.astype(BF16)


def input_work(delta, above, below, w1):
    return pl.pallas_call(
        input_body,
        out_shape=jax.ShapeDtypeStruct((PIX, C1), BF16),
        in_specs=[VMEM] * 3 + [HBM],
        out_specs=VMEM,
        scratch_shapes=[
            pltpu.VMEM((PIX + 2 * COLS, C1), BF16),
            pltpu.VMEM((3, PIX + 2 * COLS, C1), BF16),
            pltpu.VMEM((9, C1, C1), BF16),
            pltpu.SemaphoreType.DMA,
        ],
        compiler_params=pltpu.CompilerParams(vmem_limit_bytes=12 * 2**20),
        cost_estimate=pl.CostEstimate(
            flops=300_000_000, bytes_accessed=2_000_000, transcendentals=0
        ),
        name="input_work",
    )(delta, above, below, w1)


def unpack(scale_low, scale_high, code, full, first, second, bias, tiles):
    z_hi = code[0] // 8
    for half in range(2):
        for k in range(8):
            before = 2 * k - (k - z_hi + 3) // 4
            piece = full[8 * half + k].astype(F32).reshape(2, 16, 128)
            tiles[pl.ds(half * (TILES // 2) + before, 2)] = piece

    def band(n):
        return tiles[9 * n : 9 * n + 9].reshape(SLICE, 128)

    first[:, 0:C2] = band(0) * scale_low
    first[:, C2:C1] = band(1) * scale_low
    second[...] = band(2) * scale_high
    bias[...] = tiles[TILES - 1][0:1, 0:16] * scale_low


def results(code, full, scale_low, scale_high):
    return pl.pallas_call(
        lambda *refs: unpack(scale_low, scale_high, *refs),
        out_shape=(
            jax.ShapeDtypeStruct((SLICE, C1), F32),
            jax.ShapeDtypeStruct((SLICE, C2), F32),
            jax.ShapeDtypeStruct((1, 16), F32),
        ),
        in_specs=[SMEM, VMEM],
        out_specs=(VMEM,) * 3,
        scratch_shapes=[pltpu.VMEM((TILES + 1, 16, 128), F32)],
        name="unpack",
    )(code, full)


FOUR = range(4)
TWO = range(2)


def place(x, z_hi, y, zb, za, core):
    return (x * 4 + z_hi) * 32 + y * 8 + zb * 4 + za * 2 + core


BLOCK = [
    [place(x, zh, y, zb, za, c) for x in FOUR for y in FOUR for za in TWO]
    for zh in FOUR
    for zb in TWO
    for c in TWO
]
COLUMN = [
    [place(x, zh, y, zb, za, c) for zb in TWO for zh in FOUR]
    for x in FOUR
    for y in FOUR
    for za in TWO
    for c in TWO
]
SHARE = [[place(0, 0, y, zb, za, c) for c in TWO for y in FOUR for za in TWO] for zb in TWO]
QUADS = [[4 * j + b for b in FOUR] for j in range(8)]


def shards(cotangent, inputs, w_first, bias_first, w_second):
    rank = lax.axis_index("rows")
    down = [(i, i + 4) for i in range(28)]
    up = [(i + 4, i) for i in range(28)]
    both = ("dp", "rows")
    x = inputs[0]

    cot = lax.all_to_all(cotangent, "rows", 0, 0, axis_index_groups=QUADS)
    cot = cot.reshape(8, 128, C2)

    def halo(cot_rows, x_row):
        row = jnp.concatenate([x_row[:, :C2], x_row[:, C2:]], axis=0)
        return jnp.concatenate([cot_rows, row[None]])

    above = lax.ppermute(halo(cot[7:8], x[3]), "rows", down)
    below = lax.ppermute(halo(cot[0:1], x[0]), "rows", up)
    code = rank % 2 + rank // 2 % 2 * 2 + rank // 8 % 2 * 4 + lax.axis_index("dp") % 4 * 8
    code = code.astype(jnp.int32).reshape(1)
    x_flat, w1, bias, w2 = (
        pltpu.with_memory_space_constraint(value, pltpu.HBM)
        for value in (
            x.reshape(PIX, C1),
            w_first.reshape(9, C1, C1),
            bias_first.reshape(1, C1),
            w_second.reshape(9, C1, C2),
        )
    )
    cot = cot.reshape(8 * 128, C2)
    preact, w1_edge = conv_work(x_flat, w1, bias)
    boxes, grad_act, w2_edge = boxes_work(cot, w2)
    delta, delta_first, delta_last, packed, send = main_work(
        code, above, below, cot, preact, boxes, grad_act, w1_edge, w2_edge, x_flat
    )
    received = lax.ppermute(send, "rows", [(i, i ^ 1) for i in range(32)])
    from_above = lax.ppermute(delta_last, "rows", down)
    from_below = lax.ppermute(delta_first, "rows", up)

    pair = pair_work(code, packed, received)
    pair = pair.reshape(32, CHUNK, 128)
    block = lax.all_to_all(pair, both, 0, 0, axis_index_groups=BLOCK)
    block, from_above, from_below = lax.optimization_barrier((block, from_above, from_below))
    grad_x = input_work(delta, from_above, from_below, w1)
    spread = block_work(code, block).reshape((8,) + PIECE)
    column = lax.all_to_all(spread, both, 0, 0, axis_index_groups=COLUMN)
    column, grad_x = lax.optimization_barrier((column, grad_x))
    full = lax.all_to_all(column_work(column), "rows", 0, 0, axis_index_groups=SHARE)

    pixels_low = lax.axis_size("dp") * lax.axis_size("rows") * PIX
    scale_low = pixels_low ** (-0.5)
    scale_high = (4 * pixels_low) ** (-0.5)
    full = pltpu.with_memory_space_constraint(full, pltpu.VMEM)
    grad_first, grad_second, grad_bias = results(code, full, scale_low, scale_high)
    grad_input = grad_x.reshape(1, ROWS, COLS, C1)
    return grad_input, grad_first, grad_second, grad_bias.reshape(16)


def solution(mesh):
    in_specs = (P("dp", "rows", None, None), P("dp", "rows", None, None), P(), P(), P())
    out_specs = (P("dp", "rows", None, None), P("dp", None), P("dp", None), P("dp"))
    return jax.shard_map(shards, mesh=mesh, in_specs=in_specs, out_specs=out_specs, check_vma=False)
```

```python
import jax
import jax.numpy as jnp
from jax import lax
from jax.experimental import pallas as pl
from jax.experimental.pallas import tpu as pltpu
from jax.sharding import PartitionSpec as P

F32 = jnp.float32
BF16 = jnp.bfloat16
COLS = 64
C1 = 256
C2 = 128
ROWS = 4
PIX = ROWS * COLS
SLICE = 144
TILES = 28
PIECE = (32, 128)
PIECES = 16
ORDER = [
    26, 17, 11, 10, 28, 1, 5, 4, 7, 16, 9, 19, 30, 13, 22, 0,
    21, 29, 6, 12, 20, 23, 14, 15, 3, 31, 2, 24, 25, 27, 18, 8,
]
CHUNK = 16 * TILES // 4
PARTS = (CHUNK, 32, 128)


def dot(a, b, contract):
    return lax.dot_general(a, b, (contract, ((), ())), preferred_element_type=F32)


NN = ((1,), (0,))
NT = ((1,), (1,))
TN = ((0,), (0,))


def shifted(value, by):
    length = value.shape[0]
    column = lax.broadcasted_iota(jnp.int32, value.shape, 0) % COLS
    rolled = pltpu.roll(value, (-by) % length, 0)
    inside = (column + by >= 0) & (column + by < COLS)
    return jnp.where(inside, rolled, 0.0)


def tiles_of(k, z_hi):
    return 1 if k % 4 == z_hi else 2


def spot(d, tile):
    half, tile = divmod(tile, TILES // 2)
    x, z_hi = divmod(d, 4)
    k = 0
    while tile >= tiles_of(k, z_hi):
        tile -= tiles_of(k, z_hi)
        k += 1
    before = sum(tiles_of(k, z) for z in range(z_hi)) + tile
    return half, CHUNK * ORDER.index(x * 8 + k) + 16 * before


def put(packed, band, tap, value):
    for row in range(0, C1, 16):
        d, inner = divmod(tap * C1 + row, SLICE)
        half, at = spot(d, band * (SLICE // 16) + inner // 16)
        packed[half, at // 32, at % 32 : at % 32 + 16, :] = value[row : row + 16, :]


def pick_columns():
    out_row = lax.broadcasted_iota(jnp.int32, (3 * COLS, 256), 0)
    column = lax.broadcasted_iota(jnp.int32, (3 * COLS, 256), 1) % 128
    left = 2 * (out_row % COLS) + 1 - out_row // COLS
    return ((column == left) | (column == left + 1)).astype(F32).astype(BF16)


def silu_parts(preact):
    sigma = 1.0 / (1.0 + jnp.exp(-preact))
    return preact * sigma, sigma * (1.0 + preact * (1.0 - sigma))


def start(source, target, sem):
    copy = pltpu.make_async_copy(source, target, sem)
    copy.start()
    return copy


def conv_body(x_hbm, w1_hbm, bias_hbm, preact, w1_edge, xs, x, w1, bias, sems):
    x_copy = start(x_hbm, x, sems.at[0])
    bias_copy = start(bias_hbm, bias, sems.at[1])
    w1_copy = start(w1_hbm, w1, sems.at[2])
    x_copy.wait()
    wide = x[...].astype(F32)
    xs[0] = shifted(wide, -1).astype(BF16)
    xs[1] = x[...]
    xs[2] = shifted(wide, 1).astype(BF16)
    bias_copy.wait()
    w1_copy.wait()
    same = jnp.broadcast_to(bias[...], (PIX, C1))
    lower = jnp.zeros((PIX - COLS, C1), F32)
    upper = jnp.zeros((PIX - COLS, C1), F32)
    for q in range(3):
        lower = lower + dot(xs[q, 0 : PIX - COLS, :], w1[q], NN)
        same = same + dot(xs[q], w1[3 + q], NN)
        upper = upper + dot(xs[q, COLS:PIX, :], w1[6 + q], NN)
    preact[0:COLS, :] = same[0:COLS] + upper[0:COLS]
    middle = slice(COLS, PIX - COLS)
    preact[middle, :] = same[middle] + upper[COLS:] + lower[: PIX - 2 * COLS]
    preact[PIX - COLS :, :] = same[PIX - COLS :] + lower[PIX - 2 * COLS :]
    w1_edge[0:3] = w1[0:3]
    w1_edge[3:6] = w1[6:9]


def boxes_body(cot, w2_hbm, boxes, grad_act, w2_edge, w2, sem):
    w2_copy = start(w2_hbm, w2, sem)
    pick = pick_columns()
    zero = jnp.zeros((COLS, 3 * C2), BF16)
    boxes[0:COLS, 6 * C2 :] = zero
    boxes[PIX - COLS :, 0 : 3 * C2] = zero
    for h in range(7):
        sums = dot(pick, cot[128 * h : 128 * (h + 2), :], NN).astype(BF16)
        for p in range(3):
            if (h + p - 1) % 2 == 0 and 0 <= (h + p - 1) // 2 < ROWS:
                i = (h + p - 1) // 2
                for q in range(3):
                    t = 3 * p + q
                    boxes[COLS * i : COLS * (i + 1), C2 * t : C2 * (t + 1)] = sums[
                        COLS * q : COLS * (q + 1), :
                    ]
    w2_copy.wait()
    total = jnp.zeros((PIX, C1), F32)
    for t in range(9):
        total = total + dot(boxes[:, C2 * t : C2 * (t + 1)], w2[t], NT)
    grad_act[...] = total
    w2_edge[0:3] = w2[6:9]
    w2_edge[3:6] = w2[0:3]


def main_body(
    code, above, below, cot, preact_in, boxes_in, grad_act_in, w1_edge, w2_edge, x_hbm,
    delta_out, delta_first, delta_last, packed, send,
    x, boxes, ds, preact, grad_act, sems,
):
    x_copy = start(x_hbm, x.at[COLS : COLS + PIX], sems.at[1])

    boxes[...] = boxes_in[...]
    grad_act[...] = grad_act_in[...]
    preact[...] = preact_in[...]
    pick = pick_columns()
    first, last = slice(0, COLS), slice(PIX - COLS, PIX)
    for rows, p, pair in (
        (first, 2, (above[0], cot[0:128, :])),
        (last, 0, (cot[128 * 7 : 128 * 8, :], below[0])),
    ):
        sums = dot(pick, jnp.concatenate(pair), NN).astype(BF16)
        for q in range(3):
            t = 3 * p + q
            boxes[rows, C2 * t : C2 * (t + 1)] = sums[COLS * q : COLS * (q + 1), :]
    for at, halo in ((0, above), (COLS + PIX, below)):
        x[at : at + COLS, 0:C2] = halo[1, 0:COLS, :]
        x[at : at + COLS, C2:C1] = halo[1, COLS : 2 * COLS, :]
    for side, rows, p in ((0, first, 2), (1, last, 0)):
        part = grad_act[rows, :]
        for q in range(3):
            t = 3 * p + q
            part = part + dot(boxes[rows, C2 * t : C2 * (t + 1)], w2_edge[3 * side + q], NT)
        grad_act[rows, :] = part
    for side, rows, at in ((0, first, 0), (1, last, COLS + PIX)):
        wide = x[at : at + COLS, :].astype(F32)
        part = preact[rows, :]
        for q in range(3):
            part = part + dot(shifted(wide, q - 1).astype(BF16), w1_edge[3 * side + q], NN)
        preact[rows, :] = part
    act, slope = silu_parts(preact[...])
    second = dot(act.astype(BF16), boxes[...], TN).astype(BF16)
    for t in range(9):
        put(packed, 2, t, second[:, C2 * t : C2 * (t + 1)])

    delta = (grad_act[...] * slope).astype(BF16)
    delta_out[...] = delta
    delta_first[...] = delta[0:COLS]
    delta_last[...] = delta[PIX - COLS : PIX]
    wide = delta.astype(F32)
    ds[0] = shifted(wide, 1).astype(BF16)
    ds[1] = delta
    ds[2] = shifted(wide, -1).astype(BF16)

    total = jnp.sum(wide, axis=0, keepdims=True).astype(BF16).astype(F32)
    owner = lax.broadcasted_iota(jnp.int32, (16, C1), 0)
    channel = lax.broadcasted_iota(jnp.int32, (16, C1), 1)
    spread = jnp.where(channel // 16 == owner, jnp.broadcast_to(total, (16, C1)), 0.0)
    source = lax.broadcasted_iota(jnp.int32, (C1, 128), 0)
    lane = lax.broadcasted_iota(jnp.int32, (C1, 128), 1)
    fold = (source % 16 == lane).astype(F32).astype(BF16)
    folded = dot(spread.astype(BF16), fold, NN)
    row = lax.broadcasted_iota(jnp.int32, (16, 16, 128), 1)
    band = jnp.where(row == 0, jnp.broadcast_to(folded[:, None, :], (16, 16, 128)), 0.0)
    band = band.astype(BF16)
    for d in range(16):
        half, at = spot(d, TILES - 1)
        packed[half, at // 32, at % 32 : at % 32 + 16, :] = band[d]

    x_copy.wait()
    for p in range(3):
        lhs = x[p * COLS : p * COLS + PIX, :]
        for q in range(3):
            tap = 3 * p + q
            part = dot(lhs, ds[q], TN).astype(BF16)
            put(packed, 0, tap, part[:, 0:C2])
            put(packed, 1, tap, part[:, C2:C1])
    start(packed.at[1 - code[0] % 2], send, sems.at[0]).wait()


VMEM = pl.BlockSpec(memory_space=pltpu.VMEM)
HBM = pl.BlockSpec(memory_space=pltpu.HBM)
SMEM = pl.BlockSpec(memory_space=pltpu.SMEM)
ANYWHERE = pl.BlockSpec(memory_space=pl.ANY)


def conv_work(x, w1, bias):
    return pl.pallas_call(
        conv_body,
        out_shape=(
            jax.ShapeDtypeStruct((PIX, C1), F32),
            jax.ShapeDtypeStruct((6, C1, C1), BF16),
        ),
        in_specs=[HBM] * 3,
        out_specs=(VMEM, VMEM),
        scratch_shapes=[
            pltpu.VMEM((3, PIX, C1), BF16),
            pltpu.VMEM((PIX, C1), BF16),
            pltpu.VMEM((9, C1, C1), BF16),
            pltpu.VMEM((1, C1), F32),
            pltpu.SemaphoreType.DMA((3,)),
        ],
        compiler_params=pltpu.CompilerParams(vmem_limit_bytes=12 * 2**20),
        cost_estimate=pl.CostEstimate(
            flops=300_000_000, bytes_accessed=1_500_000, transcendentals=0
        ),
        name="conv_work",
    )(x, w1, bias)


def boxes_work(cot, w2):
    return pl.pallas_call(
        boxes_body,
        out_shape=(
            jax.ShapeDtypeStruct((PIX, 9 * C2), BF16),
            jax.ShapeDtypeStruct((PIX, C1), F32),
            jax.ShapeDtypeStruct((6, C1, C2), BF16),
        ),
        in_specs=[VMEM, HBM],
        out_specs=(VMEM, VMEM, VMEM),
        scratch_shapes=[pltpu.VMEM((9, C1, C2), BF16), pltpu.SemaphoreType.DMA],
        compiler_params=pltpu.CompilerParams(vmem_limit_bytes=12 * 2**20),
        cost_estimate=pl.CostEstimate(
            flops=300_000_000, bytes_accessed=1_500_000, transcendentals=0
        ),
        name="boxes_work",
    )(cot, w2)


def main_work(code, above, below, cot, preact, boxes, grad_act, w1_edge, w2_edge, x):
    return pl.pallas_call(
        main_body,
        out_shape=(
            jax.ShapeDtypeStruct((PIX, C1), BF16),
            jax.ShapeDtypeStruct((COLS, C1), BF16),
            jax.ShapeDtypeStruct((COLS, C1), BF16),
            jax.ShapeDtypeStruct((2,) + PARTS, BF16),
            jax.ShapeDtypeStruct(PARTS, BF16),
        ),
        in_specs=[SMEM] + [VMEM] * 8 + [HBM],
        out_specs=(VMEM, VMEM, VMEM, VMEM, ANYWHERE),
        scratch_shapes=[
            pltpu.VMEM((PIX + 2 * COLS, C1), BF16),
            pltpu.VMEM((PIX, 9 * C2), BF16),
            pltpu.VMEM((3, PIX, C1), BF16),
            pltpu.VMEM((PIX, C1), F32),
            pltpu.VMEM((PIX, C1), F32),
            pltpu.SemaphoreType.DMA((2,)),
        ],
        compiler_params=pltpu.CompilerParams(vmem_limit_bytes=16 * 2**20),
        cost_estimate=pl.CostEstimate(
            flops=600_000_000, bytes_accessed=5_000_000, transcendentals=70_000
        ),
        name="main_work",
    )(code, above, below, cot, preact, boxes, grad_act, w1_edge, w2_edge, x)


def pair_body(code, packed, received, pair, total, sems):
    mine = code[0] % 2
    copies = []
    for n in range(4):
        chunks = pl.ds(n * (CHUNK // 4), CHUNK // 4)
        total[chunks] = packed[mine, chunks] + received[chunks]
        copies.append(start(total.at[chunks], pair.at[chunks], sems.at[n]))
    for copy in copies:
        copy.wait()


def pair_work(code, packed, received):
    return pl.pallas_call(
        pair_body,
        out_shape=jax.ShapeDtypeStruct(PARTS, BF16),
        in_specs=[SMEM, VMEM, VMEM],
        out_specs=ANYWHERE,
        scratch_shapes=[pltpu.VMEM(PARTS, BF16), pltpu.SemaphoreType.DMA((4,))],
        compiler_params=pltpu.CompilerParams(vmem_limit_bytes=8 * 2**20),
        name="pair_work",
    )(code, packed, received)


def block_body(code, pieces, out, total):
    value = pieces[0].astype(F32)
    for n in range(1, 32):
        value = value + pieces[n].astype(F32)
    tiles = CHUNK // 16
    total[0:tiles] = value.reshape(tiles, 16, 128)
    total[tiles] = jnp.zeros((16, 128), F32)
    single = code[0] // 2 % 4
    for z_hi in range(4):
        part = total[pl.ds(2 * z_hi - jnp.where(z_hi > single, 1, 0), 2)]
        for n in range(2):
            out[n, z_hi] = part.reshape(PIECE).astype(BF16)


def block_work(code, pieces):
    return pl.pallas_call(
        block_body,
        out_shape=jax.ShapeDtypeStruct((2, 4) + PIECE, BF16),
        in_specs=[SMEM, VMEM],
        out_specs=VMEM,
        scratch_shapes=[pltpu.VMEM((TILES // 4 + 1, 16, 128), F32)],
        compiler_params=pltpu.CompilerParams(vmem_limit_bytes=4 * 2**20),
        name="block_work",
    )(code, pieces)


def column_body(pieces, out):
    total = pieces[0].astype(F32)
    for n in range(1, pieces.shape[0]):
        total = total + pieces[n].astype(F32)
    for n in range(PIECES):
        out[n] = total.astype(BF16)


def column_work(pieces):
    return pl.pallas_call(
        column_body,
        out_shape=jax.ShapeDtypeStruct((PIECES,) + PIECE, BF16),
        in_specs=[VMEM],
        out_specs=VMEM,
        compiler_params=pltpu.CompilerParams(vmem_limit_bytes=4 * 2**20),
        name="column_work",
    )(pieces)


def input_body(delta, above, below, w1_hbm, grad_x, ext, ds, w1, sem):
    w1_copy = pltpu.make_async_copy(w1_hbm, w1, sem)
    w1_copy.start()
    ext[0:COLS, :] = above[...]
    ext[COLS : COLS + PIX, :] = delta[...]
    ext[COLS + PIX :, :] = below[...]
    wide = ext[...].astype(F32)
    ds[0] = shifted(wide, 1).astype(BF16)
    ds[1] = ext[...]
    ds[2] = shifted(wide, -1).astype(BF16)
    w1_copy.wait()
    total = jnp.zeros((PIX, C1), F32)
    for p in range(3):
        for q in range(3):
            at = COLS * (2 - p)
            total = total + dot(ds[q, at : at + PIX, :], w1[3 * p + q], NT)
    grad_x[...] = total.astype(BF16)


def input_work(delta, above, below, w1):
    return pl.pallas_call(
        input_body,
        out_shape=jax.ShapeDtypeStruct((PIX, C1), BF16),
        in_specs=[VMEM] * 3 + [HBM],
        out_specs=VMEM,
        scratch_shapes=[
            pltpu.VMEM((PIX + 2 * COLS, C1), BF16),
            pltpu.VMEM((3, PIX + 2 * COLS, C1), BF16),
            pltpu.VMEM((9, C1, C1), BF16),
            pltpu.SemaphoreType.DMA,
        ],
        compiler_params=pltpu.CompilerParams(vmem_limit_bytes=12 * 2**20),
        cost_estimate=pl.CostEstimate(
            flops=300_000_000, bytes_accessed=2_000_000, transcendentals=0
        ),
        name="input_work",
    )(delta, above, below, w1)


def unpack(scale_low, scale_high, code, full, first, second, bias, tiles):
    z_hi = code[0] // 8
    for half in range(2):
        for k in range(8):
            before = 2 * k - (k - z_hi + 3) // 4
            piece = full[8 * half + k].astype(F32).reshape(2, 16, 128)
            tiles[pl.ds(half * (TILES // 2) + before, 2)] = piece

    def band(n):
        return tiles[9 * n : 9 * n + 9].reshape(SLICE, 128)

    first[:, 0:C2] = band(0) * scale_low
    first[:, C2:C1] = band(1) * scale_low
    second[...] = band(2) * scale_high
    bias[...] = tiles[TILES - 1][0:1, 0:16] * scale_low


def results(code, full, scale_low, scale_high):
    return pl.pallas_call(
        lambda *refs: unpack(scale_low, scale_high, *refs),
        out_shape=(
            jax.ShapeDtypeStruct((SLICE, C1), F32),
            jax.ShapeDtypeStruct((SLICE, C2), F32),
            jax.ShapeDtypeStruct((1, 16), F32),
        ),
        in_specs=[SMEM, VMEM],
        out_specs=(VMEM,) * 3,
        scratch_shapes=[pltpu.VMEM((TILES + 1, 16, 128), F32)],
        name="unpack",
    )(code, full)


FOUR = range(4)
TWO = range(2)


def place(x, z_hi, y, zb, za, core):
    return (x * 4 + z_hi) * 32 + y * 8 + zb * 4 + za * 2 + core


BLOCK = [
    [place(n // 8, zh, n // 2 % 4, zb, n % 2, c) for n in ORDER]
    for zh in FOUR
    for zb in TWO
    for c in TWO
]
COLUMN = [
    [place(x, zh, y, zb, za, c) for zb in TWO for zh in FOUR]
    for x in FOUR
    for y in FOUR
    for za in TWO
    for c in TWO
]
SHARE = [[place(0, 0, y, zb, za, c) for c in TWO for y in FOUR for za in TWO] for zb in TWO]
QUADS = [[4 * j + b for b in FOUR] for j in range(8)]


def shards(cotangent, inputs, w_first, bias_first, w_second):
    rank = lax.axis_index("rows")
    down = [(i, i + 4) for i in range(28)]
    up = [(i + 4, i) for i in range(28)]
    both = ("dp", "rows")
    x = inputs[0]

    cot = lax.all_to_all(cotangent, "rows", 0, 0, axis_index_groups=QUADS)
    cot = cot.reshape(8, 128, C2)

    def halo(cot_rows, x_row):
        row = jnp.concatenate([x_row[:, :C2], x_row[:, C2:]], axis=0)
        return jnp.concatenate([cot_rows, row[None]])

    above = lax.ppermute(halo(cot[7:8], x[3]), "rows", down)
    below = lax.ppermute(halo(cot[0:1], x[0]), "rows", up)
    code = rank % 2 + rank // 2 % 2 * 2 + rank // 8 % 2 * 4 + lax.axis_index("dp") % 4 * 8
    code = code.astype(jnp.int32).reshape(1)
    x_flat, w1, bias, w2 = (
        pltpu.with_memory_space_constraint(value, pltpu.HBM)
        for value in (
            x.reshape(PIX, C1),
            w_first.reshape(9, C1, C1),
            bias_first.reshape(1, C1),
            w_second.reshape(9, C1, C2),
        )
    )
    cot = cot.reshape(8 * 128, C2)
    preact, w1_edge = conv_work(x_flat, w1, bias)
    boxes, grad_act, w2_edge = boxes_work(cot, w2)
    delta, delta_first, delta_last, packed, send = main_work(
        code, above, below, cot, preact, boxes, grad_act, w1_edge, w2_edge, x_flat
    )
    received = lax.ppermute(send, "rows", [(i, i ^ 1) for i in range(32)])
    from_above = lax.ppermute(delta_last, "rows", down)
    from_below = lax.ppermute(delta_first, "rows", up)

    pair = pair_work(code, packed, received)
    pair = pair.reshape(32, CHUNK, 128)
    block = lax.all_to_all(pair, both, 0, 0, axis_index_groups=BLOCK)
    block, from_above, from_below = lax.optimization_barrier((block, from_above, from_below))
    grad_x = input_work(delta, from_above, from_below, w1)
    spread = block_work(code, block).reshape((8,) + PIECE)
    column = lax.all_to_all(spread, both, 0, 0, axis_index_groups=COLUMN)
    column, grad_x = lax.optimization_barrier((column, grad_x))
    full = lax.all_to_all(column_work(column), "rows", 0, 0, axis_index_groups=SHARE)

    pixels_low = lax.axis_size("dp") * lax.axis_size("rows") * PIX
    scale_low = pixels_low ** (-0.5)
    scale_high = (4 * pixels_low) ** (-0.5)
    full = pltpu.with_memory_space_constraint(full, pltpu.VMEM)
    grad_first, grad_second, grad_bias = results(code, full, scale_low, scale_high)
    grad_input = grad_x.reshape(1, ROWS, COLS, C1)
    return grad_input, grad_first, grad_second, grad_bias.reshape(16)


def solution(mesh):
    in_specs = (P("dp", "rows", None, None), P("dp", "rows", None, None), P(), P(), P())
    out_specs = (P("dp", "rows", None, None), P("dp", None), P("dp", None), P("dp"))
    return jax.shard_map(shards, mesh=mesh, in_specs=in_specs, out_specs=out_specs, check_vma=False)
```

```python
import jax
import jax.numpy as jnp
from jax import lax
from jax.experimental import pallas as pl
from jax.experimental.pallas import tpu as pltpu
from jax.sharding import PartitionSpec as P

F32 = jnp.float32
BF16 = jnp.bfloat16
COLS = 64
C1 = 256
C2 = 128
ROWS = 4
PIX = ROWS * COLS
SLICE = 144
TILES = 28
PIECE = (32, 128)
PIECES = 16
ORDER = [
    26, 17, 11, 10, 28, 1, 5, 4, 7, 16, 9, 19, 30, 13, 22, 0,
    21, 29, 6, 12, 20, 23, 14, 15, 3, 31, 2, 24, 25, 27, 18, 8,
]
CHUNK = 16 * TILES // 4
PARTS = (CHUNK, 32, 128)


def dot(a, b, contract):
    return lax.dot_general(a, b, (contract, ((), ())), preferred_element_type=F32)


NN = ((1,), (0,))
NT = ((1,), (1,))
TN = ((0,), (0,))


def shifted(value, by):
    length = value.shape[0]
    column = lax.broadcasted_iota(jnp.int32, value.shape, 0) % COLS
    rolled = pltpu.roll(value, (-by) % length, 0)
    inside = (column + by >= 0) & (column + by < COLS)
    return jnp.where(inside, rolled, 0.0)


def tiles_of(k, z_hi):
    return 1 if k % 4 == z_hi else 2


def spot(d, tile):
    half, tile = divmod(tile, TILES // 2)
    x, z_hi = divmod(d, 4)
    k = 0
    while tile >= tiles_of(k, z_hi):
        tile -= tiles_of(k, z_hi)
        k += 1
    before = sum(tiles_of(k, z) for z in range(z_hi)) + tile
    return half, CHUNK * ORDER.index(x * 8 + k) + 16 * before


def put(packed, band, tap, value):
    for row in range(0, C1, 16):
        d, inner = divmod(tap * C1 + row, SLICE)
        half, at = spot(d, band * (SLICE // 16) + inner // 16)
        packed[half, at // 32, at % 32 : at % 32 + 16, :] = value[row : row + 16, :]


def pick_columns():
    out_row = lax.broadcasted_iota(jnp.int32, (3 * COLS, 256), 0)
    column = lax.broadcasted_iota(jnp.int32, (3 * COLS, 256), 1) % 128
    left = 2 * (out_row % COLS) + 1 - out_row // COLS
    return ((column == left) | (column == left + 1)).astype(F32).astype(BF16)


def silu_parts(preact):
    sigma = 1.0 / (1.0 + jnp.exp(-preact))
    return preact * sigma, sigma * (1.0 + preact * (1.0 - sigma))


def start(source, target, sem):
    copy = pltpu.make_async_copy(source, target, sem)
    copy.start()
    return copy


def conv_body(x_hbm, w1_hbm, bias_hbm, preact, w1_edge, xs, x, w1, bias, sems):
    x_copy = start(x_hbm, x, sems.at[0])
    bias_copy = start(bias_hbm, bias, sems.at[1])
    w1_copy = start(w1_hbm, w1, sems.at[2])
    x_copy.wait()
    wide = x[...].astype(F32)
    xs[0] = shifted(wide, -1).astype(BF16)
    xs[1] = x[...]
    xs[2] = shifted(wide, 1).astype(BF16)
    bias_copy.wait()
    w1_copy.wait()
    same = jnp.broadcast_to(bias[...], (PIX, C1))
    lower = jnp.zeros((PIX - COLS, C1), F32)
    upper = jnp.zeros((PIX - COLS, C1), F32)
    for q in range(3):
        lower = lower + dot(xs[q, 0 : PIX - COLS, :], w1[q], NN)
        same = same + dot(xs[q], w1[3 + q], NN)
        upper = upper + dot(xs[q, COLS:PIX, :], w1[6 + q], NN)
    preact[0:COLS, :] = same[0:COLS] + upper[0:COLS]
    middle = slice(COLS, PIX - COLS)
    preact[middle, :] = same[middle] + upper[COLS:] + lower[: PIX - 2 * COLS]
    preact[PIX - COLS :, :] = same[PIX - COLS :] + lower[PIX - 2 * COLS :]
    w1_edge[0:3] = w1[0:3]
    w1_edge[3:6] = w1[6:9]


def boxes_body(cot, w2_hbm, boxes, grad_act, w2_edge, w2, sem):
    w2_copy = start(w2_hbm, w2, sem)
    pick = pick_columns()
    zero = jnp.zeros((COLS, 3 * C2), BF16)
    boxes[0:COLS, 6 * C2 :] = zero
    boxes[PIX - COLS :, 0 : 3 * C2] = zero
    for h in range(7):
        sums = dot(pick, cot[128 * h : 128 * (h + 2), :], NN).astype(BF16)
        for p in range(3):
            if (h + p - 1) % 2 == 0 and 0 <= (h + p - 1) // 2 < ROWS:
                i = (h + p - 1) // 2
                for q in range(3):
                    t = 3 * p + q
                    boxes[COLS * i : COLS * (i + 1), C2 * t : C2 * (t + 1)] = sums[
                        COLS * q : COLS * (q + 1), :
                    ]
    w2_copy.wait()
    total = jnp.zeros((PIX, C1), F32)
    for t in range(9):
        total = total + dot(boxes[:, C2 * t : C2 * (t + 1)], w2[t], NT)
    grad_act[...] = total
    w2_edge[0:3] = w2[6:9]
    w2_edge[3:6] = w2[0:3]


def main_body(
    code, above, below, cot, preact_in, boxes_in, grad_act_in, w1_edge, w2_edge, x_hbm,
    delta_out, delta_first, delta_last, packed, send,
    x, boxes, ds, preact, grad_act, sems,
):
    x_copy = start(x_hbm, x.at[COLS : COLS + PIX], sems.at[1])

    boxes[...] = boxes_in[...]
    grad_act[...] = grad_act_in[...]
    preact[...] = preact_in[...]
    pick = pick_columns()
    first, last = slice(0, COLS), slice(PIX - COLS, PIX)
    for rows, p, pair in (
        (first, 2, (above[0], cot[0:128, :])),
        (last, 0, (cot[128 * 7 : 128 * 8, :], below[0])),
    ):
        sums = dot(pick, jnp.concatenate(pair), NN).astype(BF16)
        for q in range(3):
            t = 3 * p + q
            boxes[rows, C2 * t : C2 * (t + 1)] = sums[COLS * q : COLS * (q + 1), :]
    for at, halo in ((0, above), (COLS + PIX, below)):
        x[at : at + COLS, 0:C2] = halo[1, 0:COLS, :]
        x[at : at + COLS, C2:C1] = halo[1, COLS : 2 * COLS, :]
    for side, rows, p in ((0, first, 2), (1, last, 0)):
        part = grad_act[rows, :]
        for q in range(3):
            t = 3 * p + q
            part = part + dot(boxes[rows, C2 * t : C2 * (t + 1)], w2_edge[3 * side + q], NT)
        grad_act[rows, :] = part
    for side, rows, at in ((0, first, 0), (1, last, COLS + PIX)):
        wide = x[at : at + COLS, :].astype(F32)
        part = preact[rows, :]
        for q in range(3):
            part = part + dot(shifted(wide, q - 1).astype(BF16), w1_edge[3 * side + q], NN)
        preact[rows, :] = part
    act, slope = silu_parts(preact[...])
    second = dot(act.astype(BF16), boxes[...], TN).astype(BF16)
    for t in range(9):
        put(packed, 2, t, second[:, C2 * t : C2 * (t + 1)])

    delta = (grad_act[...] * slope).astype(BF16)
    delta_out[...] = delta
    delta_first[...] = delta[0:COLS]
    delta_last[...] = delta[PIX - COLS : PIX]
    wide = delta.astype(F32)
    ds[0] = shifted(wide, 1).astype(BF16)
    ds[1] = delta
    ds[2] = shifted(wide, -1).astype(BF16)

    total = jnp.sum(wide, axis=0, keepdims=True).astype(BF16).astype(F32)
    owner = lax.broadcasted_iota(jnp.int32, (16, C1), 0)
    channel = lax.broadcasted_iota(jnp.int32, (16, C1), 1)
    spread = jnp.where(channel // 16 == owner, jnp.broadcast_to(total, (16, C1)), 0.0)
    source = lax.broadcasted_iota(jnp.int32, (C1, 128), 0)
    lane = lax.broadcasted_iota(jnp.int32, (C1, 128), 1)
    fold = (source % 16 == lane).astype(F32).astype(BF16)
    folded = dot(spread.astype(BF16), fold, NN)
    row = lax.broadcasted_iota(jnp.int32, (16, 16, 128), 1)
    band = jnp.where(row == 0, jnp.broadcast_to(folded[:, None, :], (16, 16, 128)), 0.0)
    band = band.astype(BF16)
    for d in range(16):
        half, at = spot(d, TILES - 1)
        packed[half, at // 32, at % 32 : at % 32 + 16, :] = band[d]

    x_copy.wait()
    for p in range(3):
        lhs = x[p * COLS : p * COLS + PIX, :]
        for q in range(3):
            tap = 3 * p + q
            part = dot(lhs, ds[q], TN).astype(BF16)
            put(packed, 0, tap, part[:, 0:C2])
            put(packed, 1, tap, part[:, C2:C1])
    start(packed.at[1 - code[0] % 2], send, sems.at[0]).wait()


VMEM = pl.BlockSpec(memory_space=pltpu.VMEM)
HBM = pl.BlockSpec(memory_space=pltpu.HBM)
SMEM = pl.BlockSpec(memory_space=pltpu.SMEM)
ANYWHERE = pl.BlockSpec(memory_space=pl.ANY)


def conv_work(x, w1, bias):
    return pl.pallas_call(
        conv_body,
        out_shape=(
            jax.ShapeDtypeStruct((PIX, C1), F32),
            jax.ShapeDtypeStruct((6, C1, C1), BF16),
        ),
        in_specs=[HBM] * 3,
        out_specs=(VMEM, VMEM),
        scratch_shapes=[
            pltpu.VMEM((3, PIX, C1), BF16),
            pltpu.VMEM((PIX, C1), BF16),
            pltpu.VMEM((9, C1, C1), BF16),
            pltpu.VMEM((1, C1), F32),
            pltpu.SemaphoreType.DMA((3,)),
        ],
        compiler_params=pltpu.CompilerParams(vmem_limit_bytes=12 * 2**20),
        cost_estimate=pl.CostEstimate(
            flops=300_000_000, bytes_accessed=1_500_000, transcendentals=0
        ),
        name="conv_work",
    )(x, w1, bias)


def boxes_work(cot, w2):
    return pl.pallas_call(
        boxes_body,
        out_shape=(
            jax.ShapeDtypeStruct((PIX, 9 * C2), BF16),
            jax.ShapeDtypeStruct((PIX, C1), F32),
            jax.ShapeDtypeStruct((6, C1, C2), BF16),
        ),
        in_specs=[VMEM, HBM],
        out_specs=(VMEM, VMEM, VMEM),
        scratch_shapes=[pltpu.VMEM((9, C1, C2), BF16), pltpu.SemaphoreType.DMA],
        compiler_params=pltpu.CompilerParams(vmem_limit_bytes=12 * 2**20),
        cost_estimate=pl.CostEstimate(
            flops=300_000_000, bytes_accessed=1_500_000, transcendentals=0
        ),
        name="boxes_work",
    )(cot, w2)


def main_work(code, above, below, cot, preact, boxes, grad_act, w1_edge, w2_edge, x):
    return pl.pallas_call(
        main_body,
        out_shape=(
            jax.ShapeDtypeStruct((PIX, C1), BF16),
            jax.ShapeDtypeStruct((COLS, C1), BF16),
            jax.ShapeDtypeStruct((COLS, C1), BF16),
            jax.ShapeDtypeStruct((2,) + PARTS, BF16),
            jax.ShapeDtypeStruct(PARTS, BF16),
        ),
        in_specs=[SMEM] + [VMEM] * 8 + [HBM],
        out_specs=(VMEM, VMEM, VMEM, VMEM, ANYWHERE),
        scratch_shapes=[
            pltpu.VMEM((PIX + 2 * COLS, C1), BF16),
            pltpu.VMEM((PIX, 9 * C2), BF16),
            pltpu.VMEM((3, PIX, C1), BF16),
            pltpu.VMEM((PIX, C1), F32),
            pltpu.VMEM((PIX, C1), F32),
            pltpu.SemaphoreType.DMA((2,)),
        ],
        compiler_params=pltpu.CompilerParams(vmem_limit_bytes=16 * 2**20),
        cost_estimate=pl.CostEstimate(
            flops=600_000_000, bytes_accessed=5_000_000, transcendentals=70_000
        ),
        name="main_work",
    )(code, above, below, cot, preact, boxes, grad_act, w1_edge, w2_edge, x)


def pair_body(code, packed, received, pair, total, sems):
    mine = code[0] % 2
    copies = []
    for n in range(4):
        chunks = pl.ds(n * (CHUNK // 4), CHUNK // 4)
        total[chunks] = packed[mine, chunks] + received[chunks]
        copies.append(start(total.at[chunks], pair.at[chunks], sems.at[n]))
    for copy in copies:
        copy.wait()


def pair_work(code, packed, received):
    return pl.pallas_call(
        pair_body,
        out_shape=jax.ShapeDtypeStruct(PARTS, BF16),
        in_specs=[SMEM, VMEM, VMEM],
        out_specs=ANYWHERE,
        scratch_shapes=[pltpu.VMEM(PARTS, BF16), pltpu.SemaphoreType.DMA((4,))],
        compiler_params=pltpu.CompilerParams(vmem_limit_bytes=8 * 2**20),
        name="pair_work",
    )(code, packed, received)


def block_body(code, pieces, out, total):
    value = pieces[0].astype(F32)
    for n in range(1, 32):
        value = value + pieces[n].astype(F32)
    tiles = CHUNK // 16
    total[0:tiles] = value.reshape(tiles, 16, 128)
    total[tiles] = jnp.zeros((16, 128), F32)
    single = code[0] // 2 % 4
    for z_hi in range(4):
        part = total[pl.ds(2 * z_hi - jnp.where(z_hi > single, 1, 0), 2)]
        for n, (target, _) in enumerate(Z_ORDER):
            if target == z_hi:
                out[n] = part.reshape(PIECE).astype(BF16)


def block_work(code, pieces):
    return pl.pallas_call(
        block_body,
        out_shape=jax.ShapeDtypeStruct((8,) + PIECE, BF16),
        in_specs=[SMEM, VMEM],
        out_specs=VMEM,
        scratch_shapes=[pltpu.VMEM((TILES // 4 + 1, 16, 128), F32)],
        compiler_params=pltpu.CompilerParams(vmem_limit_bytes=4 * 2**20),
        name="block_work",
    )(code, pieces)


def column_body(pieces, out):
    total = pieces[0].astype(F32)
    for n in range(1, pieces.shape[0]):
        total = total + pieces[n].astype(F32)
    for n in range(PIECES):
        out[n] = total.astype(BF16)


def column_work(pieces):
    return pl.pallas_call(
        column_body,
        out_shape=jax.ShapeDtypeStruct((PIECES,) + PIECE, BF16),
        in_specs=[VMEM],
        out_specs=VMEM,
        compiler_params=pltpu.CompilerParams(vmem_limit_bytes=4 * 2**20),
        name="column_work",
    )(pieces)


def input_body(delta, above, below, w1_hbm, grad_x, ext, ds, w1, sem):
    w1_copy = pltpu.make_async_copy(w1_hbm, w1, sem)
    w1_copy.start()
    ext[0:COLS, :] = above[...]
    ext[COLS : COLS + PIX, :] = delta[...]
    ext[COLS + PIX :, :] = below[...]
    wide = ext[...].astype(F32)
    ds[0] = shifted(wide, 1).astype(BF16)
    ds[1] = ext[...]
    ds[2] = shifted(wide, -1).astype(BF16)
    w1_copy.wait()
    total = jnp.zeros((PIX, C1), F32)
    for p in range(3):
        for q in range(3):
            at = COLS * (2 - p)
            total = total + dot(ds[q, at : at + PIX, :], w1[3 * p + q], NT)
    grad_x[...] = total.astype(BF16)


def input_work(delta, above, below, w1):
    return pl.pallas_call(
        input_body,
        out_shape=jax.ShapeDtypeStruct((PIX, C1), BF16),
        in_specs=[VMEM] * 3 + [HBM],
        out_specs=VMEM,
        scratch_shapes=[
            pltpu.VMEM((PIX + 2 * COLS, C1), BF16),
            pltpu.VMEM((3, PIX + 2 * COLS, C1), BF16),
            pltpu.VMEM((9, C1, C1), BF16),
            pltpu.SemaphoreType.DMA,
        ],
        compiler_params=pltpu.CompilerParams(vmem_limit_bytes=12 * 2**20),
        cost_estimate=pl.CostEstimate(
            flops=300_000_000, bytes_accessed=2_000_000, transcendentals=0
        ),
        name="input_work",
    )(delta, above, below, w1)


def unpack(scale_low, scale_high, code, full, first, second, bias, tiles):
    z_hi = code[0] // 8
    for half in range(2):
        for k in range(8):
            before = 2 * k - (k - z_hi + 3) // 4
            piece = full[8 * half + k].astype(F32).reshape(2, 16, 128)
            tiles[pl.ds(half * (TILES // 2) + before, 2)] = piece

    def band(n):
        return tiles[9 * n : 9 * n + 9].reshape(SLICE, 128)

    first[:, 0:C2] = band(0) * scale_low
    first[:, C2:C1] = band(1) * scale_low
    second[...] = band(2) * scale_high
    bias[...] = tiles[TILES - 1][0:1, 0:16] * scale_low


def results(code, full, scale_low, scale_high):
    return pl.pallas_call(
        lambda *refs: unpack(scale_low, scale_high, *refs),
        out_shape=(
            jax.ShapeDtypeStruct((SLICE, C1), F32),
            jax.ShapeDtypeStruct((SLICE, C2), F32),
            jax.ShapeDtypeStruct((1, 16), F32),
        ),
        in_specs=[SMEM, VMEM],
        out_specs=(VMEM,) * 3,
        scratch_shapes=[pltpu.VMEM((TILES + 1, 16, 128), F32)],
        name="unpack",
    )(code, full)


FOUR = range(4)
TWO = range(2)


def place(x, z_hi, y, zb, za, core):
    return (x * 4 + z_hi) * 32 + y * 8 + zb * 4 + za * 2 + core


BLOCK = [
    [place(n // 8, zh, n // 2 % 4, zb, n % 2, c) for n in ORDER]
    for zh in FOUR
    for zb in TWO
    for c in TWO
]
Z_ORDER = [(0, 0), (2, 0), (0, 1), (2, 1), (1, 0), (3, 0), (1, 1), (3, 1)]
COLUMN = [
    [place(x, zh, y, zb, za, c) for zh, zb in Z_ORDER]
    for x in FOUR
    for y in FOUR
    for za in TWO
    for c in TWO
]
SHARE = [[place(0, 0, y, zb, za, c) for c in TWO for y in FOUR for za in TWO] for zb in TWO]
QUADS = [[4 * j + b for b in FOUR] for j in range(8)]


def shards(cotangent, inputs, w_first, bias_first, w_second):
    rank = lax.axis_index("rows")
    down = [(i, i + 4) for i in range(28)]
    up = [(i + 4, i) for i in range(28)]
    both = ("dp", "rows")
    x = inputs[0]

    cot = lax.all_to_all(cotangent, "rows", 0, 0, axis_index_groups=QUADS)
    cot = cot.reshape(8, 128, C2)

    def halo(cot_rows, x_row):
        row = jnp.concatenate([x_row[:, :C2], x_row[:, C2:]], axis=0)
        return jnp.concatenate([cot_rows, row[None]])

    above = lax.ppermute(halo(cot[7:8], x[3]), "rows", down)
    below = lax.ppermute(halo(cot[0:1], x[0]), "rows", up)
    code = rank % 2 + rank // 2 % 2 * 2 + rank // 8 % 2 * 4 + lax.axis_index("dp") % 4 * 8
    code = code.astype(jnp.int32).reshape(1)
    x_flat, w1, bias, w2 = (
        pltpu.with_memory_space_constraint(value, pltpu.HBM)
        for value in (
            x.reshape(PIX, C1),
            w_first.reshape(9, C1, C1),
            bias_first.reshape(1, C1),
            w_second.reshape(9, C1, C2),
        )
    )
    cot = cot.reshape(8 * 128, C2)
    preact, w1_edge = conv_work(x_flat, w1, bias)
    boxes, grad_act, w2_edge = boxes_work(cot, w2)
    delta, delta_first, delta_last, packed, send = main_work(
        code, above, below, cot, preact, boxes, grad_act, w1_edge, w2_edge, x_flat
    )
    received = lax.ppermute(send, "rows", [(i, i ^ 1) for i in range(32)])
    from_above = lax.ppermute(delta_last, "rows", down)
    from_below = lax.ppermute(delta_first, "rows", up)

    pair = pair_work(code, packed, received)
    pair = pair.reshape(32, CHUNK, 128)
    block = lax.all_to_all(pair, both, 0, 0, axis_index_groups=BLOCK)
    block, from_above, from_below = lax.optimization_barrier((block, from_above, from_below))
    grad_x = input_work(delta, from_above, from_below, w1)
    spread = block_work(code, block)
    column = lax.all_to_all(spread, both, 0, 0, axis_index_groups=COLUMN)
    column, grad_x = lax.optimization_barrier((column, grad_x))
    full = lax.all_to_all(column_work(column), "rows", 0, 0, axis_index_groups=SHARE)

    pixels_low = lax.axis_size("dp") * lax.axis_size("rows") * PIX
    scale_low = pixels_low ** (-0.5)
    scale_high = (4 * pixels_low) ** (-0.5)
    full = pltpu.with_memory_space_constraint(full, pltpu.VMEM)
    grad_first, grad_second, grad_bias = results(code, full, scale_low, scale_high)
    grad_input = grad_x.reshape(1, ROWS, COLS, C1)
    return grad_input, grad_first, grad_second, grad_bias.reshape(16)


def solution(mesh):
    in_specs = (P("dp", "rows", None, None), P("dp", "rows", None, None), P(), P(), P())
    out_specs = (P("dp", "rows", None, None), P("dp", None), P("dp", None), P("dp"))
    return jax.shard_map(shards, mesh=mesh, in_specs=in_specs, out_specs=out_specs, check_vma=False)
```

```python
import jax
import jax.numpy as jnp
from jax import lax
from jax.experimental import pallas as pl
from jax.experimental.pallas import tpu as pltpu
from jax.sharding import PartitionSpec as P

F32 = jnp.float32
BF16 = jnp.bfloat16
COLS = 64
C1 = 256
C2 = 128
ROWS = 4
PIX = ROWS * COLS
SLICE = 144
TILES = 28
PIECE = (32, 128)
PIECES = 16
ORDER = [
    26, 17, 11, 10, 28, 1, 5, 4, 7, 16, 9, 19, 30, 13, 22, 0,
    21, 29, 6, 12, 20, 23, 14, 15, 3, 31, 2, 24, 25, 27, 18, 8,
]
CHUNK = 16 * TILES // 4
PARTS = (CHUNK, 32, 128)


def dot(a, b, contract):
    return lax.dot_general(a, b, (contract, ((), ())), preferred_element_type=F32)


NN = ((1,), (0,))
NT = ((1,), (1,))
TN = ((0,), (0,))


def shifted(value, by):
    length = value.shape[0]
    column = lax.broadcasted_iota(jnp.int32, value.shape, 0) % COLS
    rolled = pltpu.roll(value, (-by) % length, 0)
    inside = (column + by >= 0) & (column + by < COLS)
    return jnp.where(inside, rolled, 0.0)


def tiles_of(k, z_hi):
    return 1 if k % 4 == z_hi else 2


def spot(d, tile):
    half, tile = divmod(tile, TILES // 2)
    x, z_hi = divmod(d, 4)
    k = 0
    while tile >= tiles_of(k, z_hi):
        tile -= tiles_of(k, z_hi)
        k += 1
    before = sum(tiles_of(k, z) for z in range(z_hi)) + tile
    return half, CHUNK * ORDER.index(x * 8 + k) + 16 * before


def put(packed, band, tap, value):
    for row in range(0, C1, 16):
        d, inner = divmod(tap * C1 + row, SLICE)
        half, at = spot(d, band * (SLICE // 16) + inner // 16)
        packed[half, at // 32, at % 32 : at % 32 + 16, :] = value[row : row + 16, :]


def pick_columns():
    out_row = lax.broadcasted_iota(jnp.int32, (3 * COLS, 256), 0)
    column = lax.broadcasted_iota(jnp.int32, (3 * COLS, 256), 1) % 128
    left = 2 * (out_row % COLS) + 1 - out_row // COLS
    return ((column == left) | (column == left + 1)).astype(F32).astype(BF16)


def silu_parts(preact):
    sigma = 1.0 / (1.0 + jnp.exp(-preact))
    return preact * sigma, sigma * (1.0 + preact * (1.0 - sigma))


def start(source, target, sem):
    copy = pltpu.make_async_copy(source, target, sem)
    copy.start()
    return copy


def conv_body(x_hbm, w1_hbm, bias_hbm, preact, w1_edge, xs, x, w1, bias, sems):
    x_copy = start(x_hbm, x, sems.at[0])
    bias_copy = start(bias_hbm, bias, sems.at[1])
    w1_copy = start(w1_hbm, w1, sems.at[2])
    x_copy.wait()
    wide = x[...].astype(F32)
    xs[0] = shifted(wide, -1).astype(BF16)
    xs[1] = x[...]
    xs[2] = shifted(wide, 1).astype(BF16)
    bias_copy.wait()
    w1_copy.wait()
    same = jnp.broadcast_to(bias[...], (PIX, C1))
    lower = jnp.zeros((PIX - COLS, C1), F32)
    upper = jnp.zeros((PIX - COLS, C1), F32)
    for q in range(3):
        lower = lower + dot(xs[q, 0 : PIX - COLS, :], w1[q], NN)
        same = same + dot(xs[q], w1[3 + q], NN)
        upper = upper + dot(xs[q, COLS:PIX, :], w1[6 + q], NN)
    preact[0:COLS, :] = same[0:COLS] + upper[0:COLS]
    middle = slice(COLS, PIX - COLS)
    preact[middle, :] = same[middle] + upper[COLS:] + lower[: PIX - 2 * COLS]
    preact[PIX - COLS :, :] = same[PIX - COLS :] + lower[PIX - 2 * COLS :]
    w1_edge[0:3] = w1[0:3]
    w1_edge[3:6] = w1[6:9]


def boxes_body(cot, w2_hbm, boxes, grad_act, w2_edge, w2, sem):
    w2_copy = start(w2_hbm, w2, sem)
    pick = pick_columns()
    zero = jnp.zeros((COLS, 3 * C2), BF16)
    boxes[0:COLS, 6 * C2 :] = zero
    boxes[PIX - COLS :, 0 : 3 * C2] = zero
    for h in range(7):
        sums = dot(pick, cot[128 * h : 128 * (h + 2), :], NN).astype(BF16)
        for p in range(3):
            if (h + p - 1) % 2 == 0 and 0 <= (h + p - 1) // 2 < ROWS:
                i = (h + p - 1) // 2
                for q in range(3):
                    t = 3 * p + q
                    boxes[COLS * i : COLS * (i + 1), C2 * t : C2 * (t + 1)] = sums[
                        COLS * q : COLS * (q + 1), :
                    ]
    w2_copy.wait()
    total = jnp.zeros((PIX, C1), F32)
    for t in range(9):
        total = total + dot(boxes[:, C2 * t : C2 * (t + 1)], w2[t], NT)
    grad_act[...] = total
    w2_edge[0:3] = w2[6:9]
    w2_edge[3:6] = w2[0:3]


def main_body(
    code, above, below, cot, preact_in, boxes_in, grad_act_in, w1_edge, w2_edge, x_hbm,
    delta_out, delta_first, delta_last, packed, send,
    x, boxes, ds, preact, grad_act, sems,
):
    x_copy = start(x_hbm, x.at[COLS : COLS + PIX], sems.at[1])

    boxes[...] = boxes_in[...]
    grad_act[...] = grad_act_in[...]
    preact[...] = preact_in[...]
    pick = pick_columns()
    first, last = slice(0, COLS), slice(PIX - COLS, PIX)
    for rows, p, pair in (
        (first, 2, (above[0], cot[0:128, :])),
        (last, 0, (cot[128 * 7 : 128 * 8, :], below[0])),
    ):
        sums = dot(pick, jnp.concatenate(pair), NN).astype(BF16)
        for q in range(3):
            t = 3 * p + q
            boxes[rows, C2 * t : C2 * (t + 1)] = sums[COLS * q : COLS * (q + 1), :]
    for at, halo in ((0, above), (COLS + PIX, below)):
        x[at : at + COLS, 0:C2] = halo[1, 0:COLS, :]
        x[at : at + COLS, C2:C1] = halo[1, COLS : 2 * COLS, :]
    for side, rows, p in ((0, first, 2), (1, last, 0)):
        part = grad_act[rows, :]
        for q in range(3):
            t = 3 * p + q
            part = part + dot(boxes[rows, C2 * t : C2 * (t + 1)], w2_edge[3 * side + q], NT)
        grad_act[rows, :] = part
    for side, rows, at in ((0, first, 0), (1, last, COLS + PIX)):
        wide = x[at : at + COLS, :].astype(F32)
        part = preact[rows, :]
        for q in range(3):
            part = part + dot(shifted(wide, q - 1).astype(BF16), w1_edge[3 * side + q], NN)
        preact[rows, :] = part
    act, slope = silu_parts(preact[...])
    second = dot(act.astype(BF16), boxes[...], TN).astype(BF16)
    for t in range(9):
        put(packed, 2, t, second[:, C2 * t : C2 * (t + 1)])

    delta = (grad_act[...] * slope).astype(BF16)
    delta_out[...] = delta
    delta_first[...] = delta[0:COLS]
    delta_last[...] = delta[PIX - COLS : PIX]
    wide = delta.astype(F32)
    ds[0] = shifted(wide, 1).astype(BF16)
    ds[1] = delta
    ds[2] = shifted(wide, -1).astype(BF16)

    total = jnp.sum(wide, axis=0, keepdims=True).astype(BF16).astype(F32)
    owner = lax.broadcasted_iota(jnp.int32, (16, C1), 0)
    channel = lax.broadcasted_iota(jnp.int32, (16, C1), 1)
    spread = jnp.where(channel // 16 == owner, jnp.broadcast_to(total, (16, C1)), 0.0)
    source = lax.broadcasted_iota(jnp.int32, (C1, 128), 0)
    lane = lax.broadcasted_iota(jnp.int32, (C1, 128), 1)
    fold = (source % 16 == lane).astype(F32).astype(BF16)
    folded = dot(spread.astype(BF16), fold, NN)
    row = lax.broadcasted_iota(jnp.int32, (16, 16, 128), 1)
    band = jnp.where(row == 0, jnp.broadcast_to(folded[:, None, :], (16, 16, 128)), 0.0)
    band = band.astype(BF16)
    for d in range(16):
        half, at = spot(d, TILES - 1)
        packed[half, at // 32, at % 32 : at % 32 + 16, :] = band[d]

    x_copy.wait()
    for p in range(3):
        lhs = x[p * COLS : p * COLS + PIX, :]
        for q in range(3):
            tap = 3 * p + q
            part = dot(lhs, ds[q], TN).astype(BF16)
            put(packed, 0, tap, part[:, 0:C2])
            put(packed, 1, tap, part[:, C2:C1])
    start(packed.at[1 - code[0] % 2], send, sems.at[0]).wait()


VMEM = pl.BlockSpec(memory_space=pltpu.VMEM)
HBM = pl.BlockSpec(memory_space=pltpu.HBM)
SMEM = pl.BlockSpec(memory_space=pltpu.SMEM)
ANYWHERE = pl.BlockSpec(memory_space=pl.ANY)


def conv_work(x, w1, bias):
    return pl.pallas_call(
        conv_body,
        out_shape=(
            jax.ShapeDtypeStruct((PIX, C1), F32),
            jax.ShapeDtypeStruct((6, C1, C1), BF16),
        ),
        in_specs=[HBM] * 3,
        out_specs=(VMEM, VMEM),
        scratch_shapes=[
            pltpu.VMEM((3, PIX, C1), BF16),
            pltpu.VMEM((PIX, C1), BF16),
            pltpu.VMEM((9, C1, C1), BF16),
            pltpu.VMEM((1, C1), F32),
            pltpu.SemaphoreType.DMA((3,)),
        ],
        compiler_params=pltpu.CompilerParams(vmem_limit_bytes=12 * 2**20),
        cost_estimate=pl.CostEstimate(
            flops=300_000_000, bytes_accessed=1_500_000, transcendentals=0
        ),
        name="conv_work",
    )(x, w1, bias)


def boxes_work(cot, w2):
    return pl.pallas_call(
        boxes_body,
        out_shape=(
            jax.ShapeDtypeStruct((PIX, 9 * C2), BF16),
            jax.ShapeDtypeStruct((PIX, C1), F32),
            jax.ShapeDtypeStruct((6, C1, C2), BF16),
        ),
        in_specs=[VMEM, HBM],
        out_specs=(VMEM, VMEM, VMEM),
        scratch_shapes=[pltpu.VMEM((9, C1, C2), BF16), pltpu.SemaphoreType.DMA],
        compiler_params=pltpu.CompilerParams(vmem_limit_bytes=12 * 2**20),
        cost_estimate=pl.CostEstimate(
            flops=300_000_000, bytes_accessed=1_500_000, transcendentals=0
        ),
        name="boxes_work",
    )(cot, w2)


def main_work(code, above, below, cot, preact, boxes, grad_act, w1_edge, w2_edge, x):
    return pl.pallas_call(
        main_body,
        out_shape=(
            jax.ShapeDtypeStruct((PIX, C1), BF16),
            jax.ShapeDtypeStruct((COLS, C1), BF16),
            jax.ShapeDtypeStruct((COLS, C1), BF16),
            jax.ShapeDtypeStruct((2,) + PARTS, BF16),
            jax.ShapeDtypeStruct(PARTS, BF16),
        ),
        in_specs=[SMEM] + [VMEM] * 8 + [HBM],
        out_specs=(VMEM, VMEM, VMEM, VMEM, ANYWHERE),
        scratch_shapes=[
            pltpu.VMEM((PIX + 2 * COLS, C1), BF16),
            pltpu.VMEM((PIX, 9 * C2), BF16),
            pltpu.VMEM((3, PIX, C1), BF16),
            pltpu.VMEM((PIX, C1), F32),
            pltpu.VMEM((PIX, C1), F32),
            pltpu.SemaphoreType.DMA((2,)),
        ],
        compiler_params=pltpu.CompilerParams(vmem_limit_bytes=16 * 2**20),
        cost_estimate=pl.CostEstimate(
            flops=600_000_000, bytes_accessed=5_000_000, transcendentals=70_000
        ),
        name="main_work",
    )(code, above, below, cot, preact, boxes, grad_act, w1_edge, w2_edge, x)


def pair_body(code, packed, received, pair, total, sems):
    mine = code[0] % 2
    copies = []
    for n in range(4):
        chunks = pl.ds(n * (CHUNK // 4), CHUNK // 4)
        total[chunks] = packed[mine, chunks] + received[chunks]
        copies.append(start(total.at[chunks], pair.at[chunks], sems.at[n]))
    for copy in copies:
        copy.wait()


def pair_work(code, packed, received):
    return pl.pallas_call(
        pair_body,
        out_shape=jax.ShapeDtypeStruct(PARTS, BF16),
        in_specs=[SMEM, VMEM, VMEM],
        out_specs=ANYWHERE,
        scratch_shapes=[pltpu.VMEM(PARTS, BF16), pltpu.SemaphoreType.DMA((4,))],
        compiler_params=pltpu.CompilerParams(vmem_limit_bytes=8 * 2**20),
        name="pair_work",
    )(code, packed, received)


def block_body(code, pieces, out, total):
    value = pieces[0].astype(F32)
    for n in range(1, 32):
        value = value + pieces[n].astype(F32)
    tiles = CHUNK // 16
    total[0:tiles] = value.reshape(tiles, 16, 128)
    total[tiles] = jnp.zeros((16, 128), F32)
    single = code[0] // 2 % 4
    for z_hi in range(4):
        part = total[pl.ds(2 * z_hi - jnp.where(z_hi > single, 1, 0), 2)]
        for n, (target, _) in enumerate(Z_ORDER):
            if target == z_hi:
                out[n] = part.reshape(PIECE).astype(BF16)


def block_work(code, pieces):
    return pl.pallas_call(
        block_body,
        out_shape=jax.ShapeDtypeStruct((8,) + PIECE, BF16),
        in_specs=[SMEM, VMEM],
        out_specs=VMEM,
        scratch_shapes=[pltpu.VMEM((TILES // 4 + 1, 16, 128), F32)],
        compiler_params=pltpu.CompilerParams(vmem_limit_bytes=4 * 2**20),
        name="block_work",
    )(code, pieces)


def column_body(pieces, out):
    total = pieces[0].astype(F32)
    for n in range(1, pieces.shape[0]):
        total = total + pieces[n].astype(F32)
    for n in range(PIECES):
        out[n] = total.astype(BF16)


def column_work(pieces):
    return pl.pallas_call(
        column_body,
        out_shape=jax.ShapeDtypeStruct((PIECES,) + PIECE, BF16),
        in_specs=[VMEM],
        out_specs=VMEM,
        compiler_params=pltpu.CompilerParams(vmem_limit_bytes=4 * 2**20),
        name="column_work",
    )(pieces)


def input_body(delta, above, below, w1_hbm, grad_x, ext, ds, w1, sem):
    w1_copy = pltpu.make_async_copy(w1_hbm, w1, sem)
    w1_copy.start()
    ext[0:COLS, :] = above[...]
    ext[COLS : COLS + PIX, :] = delta[...]
    ext[COLS + PIX :, :] = below[...]
    wide = ext[...].astype(F32)
    ds[0] = shifted(wide, 1).astype(BF16)
    ds[1] = ext[...]
    ds[2] = shifted(wide, -1).astype(BF16)
    w1_copy.wait()
    total = jnp.zeros((PIX, C1), F32)
    for p in range(3):
        for q in range(3):
            at = COLS * (2 - p)
            total = total + dot(ds[q, at : at + PIX, :], w1[3 * p + q], NT)
    grad_x[...] = total.astype(BF16)


def input_work(delta, above, below, w1):
    return pl.pallas_call(
        input_body,
        out_shape=jax.ShapeDtypeStruct((PIX, C1), BF16),
        in_specs=[VMEM] * 3 + [HBM],
        out_specs=VMEM,
        scratch_shapes=[
            pltpu.VMEM((PIX + 2 * COLS, C1), BF16),
            pltpu.VMEM((3, PIX + 2 * COLS, C1), BF16),
            pltpu.VMEM((9, C1, C1), BF16),
            pltpu.SemaphoreType.DMA,
        ],
        compiler_params=pltpu.CompilerParams(vmem_limit_bytes=12 * 2**20),
        cost_estimate=pl.CostEstimate(
            flops=300_000_000, bytes_accessed=2_000_000, transcendentals=0
        ),
        name="input_work",
    )(delta, above, below, w1)


def unpack(scale_low, scale_high, code, full, first, second, bias, tiles):
    z_hi = code[0] // 8
    for half in range(2):
        for k in range(8):
            before = 2 * k - (k - z_hi + 3) // 4
            piece = full[8 * half + k].astype(F32).reshape(2, 16, 128)
            tiles[pl.ds(half * (TILES // 2) + before, 2)] = piece

    def band(n):
        return tiles[9 * n : 9 * n + 9].reshape(SLICE, 128)

    first[:, 0:C2] = band(0) * scale_low
    first[:, C2:C1] = band(1) * scale_low
    second[...] = band(2) * scale_high
    bias[...] = tiles[TILES - 1][0:1, 0:16] * scale_low


def results(code, full, scale_low, scale_high):
    return pl.pallas_call(
        lambda *refs: unpack(scale_low, scale_high, *refs),
        out_shape=(
            jax.ShapeDtypeStruct((SLICE, C1), F32),
            jax.ShapeDtypeStruct((SLICE, C2), F32),
            jax.ShapeDtypeStruct((1, 16), F32),
        ),
        in_specs=[SMEM, VMEM],
        out_specs=(VMEM,) * 3,
        scratch_shapes=[pltpu.VMEM((TILES + 1, 16, 128), F32)],
        name="unpack",
    )(code, full)


FOUR = range(4)
TWO = range(2)


def place(x, z_hi, y, zb, za, core):
    return (x * 4 + z_hi) * 32 + y * 8 + zb * 4 + za * 2 + core


BLOCK = [
    [place(n // 8, zh, n // 2 % 4, zb, n % 2, c) for n in ORDER]
    for zh in FOUR
    for zb in TWO
    for c in TWO
]
Z_ORDER = [(0, 0), (2, 0), (0, 1), (2, 1), (1, 0), (3, 0), (1, 1), (3, 1)]
COLUMN = [
    [place(x, zh, y, zb, za, c) for zh, zb in Z_ORDER]
    for x in FOUR
    for y in FOUR
    for za in TWO
    for c in TWO
]
SHARE = [[place(0, 0, y, zb, za, c) for c in TWO for y in FOUR for za in TWO] for zb in TWO]
QUADS = [[4 * j + b for b in FOUR] for j in range(8)]


def shards(cotangent, inputs, w_first, bias_first, w_second):
    rank = lax.axis_index("rows")
    down = [(i, i + 4) for i in range(28)]
    up = [(i + 4, i) for i in range(28)]
    both = ("dp", "rows")
    x = inputs[0]

    cot = lax.all_to_all(cotangent, "rows", 0, 0, axis_index_groups=QUADS)
    cot = cot.reshape(8, 128, C2)

    x_flat, w1, bias, w2 = (
        pltpu.with_memory_space_constraint(value, pltpu.HBM)
        for value in (
            x.reshape(PIX, C1),
            w_first.reshape(9, C1, C1),
            bias_first.reshape(1, C1),
            w_second.reshape(9, C1, C2),
        )
    )
    preact, w1_edge = conv_work(x_flat, w1, bias)
    cot, preact = lax.optimization_barrier((cot, preact))

    def halo(cot_rows, x_row):
        row = jnp.concatenate([x_row[:, :C2], x_row[:, C2:]], axis=0)
        return jnp.concatenate([cot_rows, row[None]])

    above = lax.ppermute(halo(cot[7:8], x[3]), "rows", down)
    below = lax.ppermute(halo(cot[0:1], x[0]), "rows", up)
    code = rank % 2 + rank // 2 % 2 * 2 + rank // 8 % 2 * 4 + lax.axis_index("dp") % 4 * 8
    code = code.astype(jnp.int32).reshape(1)
    cot = cot.reshape(8 * 128, C2)
    boxes, grad_act, w2_edge = boxes_work(cot, w2)
    delta, delta_first, delta_last, packed, send = main_work(
        code, above, below, cot, preact, boxes, grad_act, w1_edge, w2_edge, x_flat
    )
    received = lax.ppermute(send, "rows", [(i, i ^ 1) for i in range(32)])
    from_above = lax.ppermute(delta_last, "rows", down)
    from_below = lax.ppermute(delta_first, "rows", up)

    pair = pair_work(code, packed, received)
    pair = pair.reshape(32, CHUNK, 128)
    block = lax.all_to_all(pair, both, 0, 0, axis_index_groups=BLOCK)
    block, from_above, from_below = lax.optimization_barrier((block, from_above, from_below))
    grad_x = input_work(delta, from_above, from_below, w1)
    spread = block_work(code, block)
    column = lax.all_to_all(spread, both, 0, 0, axis_index_groups=COLUMN)
    column, grad_x = lax.optimization_barrier((column, grad_x))
    full = lax.all_to_all(column_work(column), "rows", 0, 0, axis_index_groups=SHARE)

    pixels_low = lax.axis_size("dp") * lax.axis_size("rows") * PIX
    scale_low = pixels_low ** (-0.5)
    scale_high = (4 * pixels_low) ** (-0.5)
    full = pltpu.with_memory_space_constraint(full, pltpu.VMEM)
    grad_first, grad_second, grad_bias = results(code, full, scale_low, scale_high)
    grad_input = grad_x.reshape(1, ROWS, COLS, C1)
    return grad_input, grad_first, grad_second, grad_bias.reshape(16)


def solution(mesh):
    in_specs = (P("dp", "rows", None, None), P("dp", "rows", None, None), P(), P(), P())
    out_specs = (P("dp", "rows", None, None), P("dp", None), P("dp", None), P("dp"))
    return jax.shard_map(shards, mesh=mesh, in_specs=in_specs, out_specs=out_specs, check_vma=False)
```

```python
import jax
import jax.numpy as jnp
from jax import lax
from jax.experimental import pallas as pl
from jax.experimental.pallas import tpu as pltpu
from jax.sharding import PartitionSpec as P

F32 = jnp.float32
BF16 = jnp.bfloat16
COLS = 64
C1 = 256
C2 = 128
ROWS = 4
PIX = ROWS * COLS
SLICE = 144
TILES = 28
PIECE = (32, 128)
PIECES = 16
ORDER = [
    26, 17, 11, 10, 28, 1, 5, 4, 7, 16, 9, 19, 30, 13, 22, 0,
    21, 29, 6, 12, 20, 23, 14, 15, 3, 31, 2, 24, 25, 27, 18, 8,
]
CHUNK = 16 * TILES // 4
PARTS = (CHUNK, 32, 128)


def dot(a, b, contract):
    return lax.dot_general(a, b, (contract, ((), ())), preferred_element_type=F32)


NN = ((1,), (0,))
NT = ((1,), (1,))
TN = ((0,), (0,))


def shifted(value, by):
    length = value.shape[0]
    column = lax.broadcasted_iota(jnp.int32, value.shape, 0) % COLS
    rolled = pltpu.roll(value, (-by) % length, 0)
    inside = (column + by >= 0) & (column + by < COLS)
    return jnp.where(inside, rolled, 0.0)


def tiles_of(k, z_hi):
    return 1 if k % 4 == z_hi else 2


def spot(d, tile):
    half, tile = divmod(tile, TILES // 2)
    x, z_hi = divmod(d, 4)
    k = 0
    while tile >= tiles_of(k, z_hi):
        tile -= tiles_of(k, z_hi)
        k += 1
    before = sum(tiles_of(k, z) for z in range(z_hi)) + tile
    return half, CHUNK * ORDER.index(x * 8 + k) + 16 * before


def put(packed, band, tap, value):
    for row in range(0, C1, 16):
        d, inner = divmod(tap * C1 + row, SLICE)
        half, at = spot(d, band * (SLICE // 16) + inner // 16)
        packed[half, at // 32, at % 32 : at % 32 + 16, :] = value[row : row + 16, :]


def pick_columns():
    out_row = lax.broadcasted_iota(jnp.int32, (3 * COLS, 256), 0)
    column = lax.broadcasted_iota(jnp.int32, (3 * COLS, 256), 1) % 128
    left = 2 * (out_row % COLS) + 1 - out_row // COLS
    return ((column == left) | (column == left + 1)).astype(F32).astype(BF16)


def silu_parts(preact):
    sigma = 1.0 / (1.0 + jnp.exp(-preact))
    return preact * sigma, sigma * (1.0 + preact * (1.0 - sigma))


def start(source, target, sem):
    copy = pltpu.make_async_copy(source, target, sem)
    copy.start()
    return copy


def conv_body(x_hbm, w1_hbm, bias_hbm, preact, w1_edge, xs, x, w1, bias, sems):
    x_copy = start(x_hbm, x, sems.at[0])
    bias_copy = start(bias_hbm, bias, sems.at[1])
    w1_copy = start(w1_hbm, w1, sems.at[2])
    x_copy.wait()
    wide = x[...].astype(F32)
    xs[0] = shifted(wide, -1).astype(BF16)
    xs[1] = x[...]
    xs[2] = shifted(wide, 1).astype(BF16)
    bias_copy.wait()
    w1_copy.wait()
    same = jnp.broadcast_to(bias[...], (PIX, C1))
    lower = jnp.zeros((PIX - COLS, C1), F32)
    upper = jnp.zeros((PIX - COLS, C1), F32)
    for q in range(3):
        lower = lower + dot(xs[q, 0 : PIX - COLS, :], w1[q], NN)
        same = same + dot(xs[q], w1[3 + q], NN)
        upper = upper + dot(xs[q, COLS:PIX, :], w1[6 + q], NN)
    preact[0:COLS, :] = same[0:COLS] + upper[0:COLS]
    middle = slice(COLS, PIX - COLS)
    preact[middle, :] = same[middle] + upper[COLS:] + lower[: PIX - 2 * COLS]
    preact[PIX - COLS :, :] = same[PIX - COLS :] + lower[PIX - 2 * COLS :]
    w1_edge[0:3] = w1[0:3]
    w1_edge[3:6] = w1[6:9]


def boxes_body(cot, w2_hbm, boxes, grad_act, w2_edge, w2, sem):
    w2_copy = start(w2_hbm, w2, sem)
    pick = pick_columns()
    zero = jnp.zeros((COLS, 3 * C2), BF16)
    boxes[0:COLS, 6 * C2 :] = zero
    boxes[PIX - COLS :, 0 : 3 * C2] = zero
    for h in range(7):
        sums = dot(pick, cot[128 * h : 128 * (h + 2), :], NN).astype(BF16)
        for p in range(3):
            if (h + p - 1) % 2 == 0 and 0 <= (h + p - 1) // 2 < ROWS:
                i = (h + p - 1) // 2
                for q in range(3):
                    t = 3 * p + q
                    boxes[COLS * i : COLS * (i + 1), C2 * t : C2 * (t + 1)] = sums[
                        COLS * q : COLS * (q + 1), :
                    ]
    w2_copy.wait()
    total = jnp.zeros((PIX, C1), F32)
    for t in range(9):
        total = total + dot(boxes[:, C2 * t : C2 * (t + 1)], w2[t], NT)
    grad_act[...] = total
    w2_edge[0:3] = w2[6:9]
    w2_edge[3:6] = w2[0:3]


def main_body(
    code, above, below, cot, preact_in, boxes_in, grad_act_in, w1_edge, w2_edge, x_hbm,
    delta_out, delta_first, delta_last, packed, send,
    x, boxes, ds, preact, grad_act, sems,
):
    x_copy = start(x_hbm, x.at[COLS : COLS + PIX], sems.at[1])

    boxes[...] = boxes_in[...]
    grad_act[...] = grad_act_in[...]
    preact[...] = preact_in[...]
    pick = pick_columns()
    first, last = slice(0, COLS), slice(PIX - COLS, PIX)
    for rows, p, pair in (
        (first, 2, (above[0], cot[0:128, :])),
        (last, 0, (cot[128 * 7 : 128 * 8, :], below[0])),
    ):
        sums = dot(pick, jnp.concatenate(pair), NN).astype(BF16)
        for q in range(3):
            t = 3 * p + q
            boxes[rows, C2 * t : C2 * (t + 1)] = sums[COLS * q : COLS * (q + 1), :]
    for at, halo in ((0, above), (COLS + PIX, below)):
        x[at : at + COLS, 0:C2] = halo[1, 0:COLS, :]
        x[at : at + COLS, C2:C1] = halo[1, COLS : 2 * COLS, :]
    for side, rows, p in ((0, first, 2), (1, last, 0)):
        part = grad_act[rows, :]
        for q in range(3):
            t = 3 * p + q
            part = part + dot(boxes[rows, C2 * t : C2 * (t + 1)], w2_edge[3 * side + q], NT)
        grad_act[rows, :] = part
    for side, rows, at in ((0, first, 0), (1, last, COLS + PIX)):
        wide = x[at : at + COLS, :].astype(F32)
        part = preact[rows, :]
        for q in range(3):
            part = part + dot(shifted(wide, q - 1).astype(BF16), w1_edge[3 * side + q], NN)
        preact[rows, :] = part
    act, slope = silu_parts(preact[...])
    second = dot(act.astype(BF16), boxes[...], TN).astype(BF16)
    for t in range(9):
        put(packed, 2, t, second[:, C2 * t : C2 * (t + 1)])

    delta = (grad_act[...] * slope).astype(BF16)
    delta_out[...] = delta
    delta_first[...] = delta[0:COLS]
    delta_last[...] = delta[PIX - COLS : PIX]
    wide = delta.astype(F32)
    ds[0] = shifted(wide, 1).astype(BF16)
    ds[1] = delta
    ds[2] = shifted(wide, -1).astype(BF16)

    total = jnp.sum(wide, axis=0, keepdims=True).astype(BF16).astype(F32)
    owner = lax.broadcasted_iota(jnp.int32, (16, C1), 0)
    channel = lax.broadcasted_iota(jnp.int32, (16, C1), 1)
    spread = jnp.where(channel // 16 == owner, jnp.broadcast_to(total, (16, C1)), 0.0)
    source = lax.broadcasted_iota(jnp.int32, (C1, 128), 0)
    lane = lax.broadcasted_iota(jnp.int32, (C1, 128), 1)
    fold = (source % 16 == lane).astype(F32).astype(BF16)
    folded = dot(spread.astype(BF16), fold, NN)
    row = lax.broadcasted_iota(jnp.int32, (16, 16, 128), 1)
    band = jnp.where(row == 0, jnp.broadcast_to(folded[:, None, :], (16, 16, 128)), 0.0)
    band = band.astype(BF16)
    for d in range(16):
        half, at = spot(d, TILES - 1)
        packed[half, at // 32, at % 32 : at % 32 + 16, :] = band[d]

    x_copy.wait()
    for p in range(3):
        lhs = x[p * COLS : p * COLS + PIX, :]
        for q in range(3):
            tap = 3 * p + q
            part = dot(lhs, ds[q], TN).astype(BF16)
            put(packed, 0, tap, part[:, 0:C2])
            put(packed, 1, tap, part[:, C2:C1])
    start(packed.at[1 - code[0] % 2], send, sems.at[0]).wait()


VMEM = pl.BlockSpec(memory_space=pltpu.VMEM)
HBM = pl.BlockSpec(memory_space=pltpu.HBM)
SMEM = pl.BlockSpec(memory_space=pltpu.SMEM)
ANYWHERE = pl.BlockSpec(memory_space=pl.ANY)


def conv_work(x, w1, bias):
    return pl.pallas_call(
        conv_body,
        out_shape=(
            jax.ShapeDtypeStruct((PIX, C1), F32),
            jax.ShapeDtypeStruct((6, C1, C1), BF16),
        ),
        in_specs=[HBM] * 3,
        out_specs=(VMEM, VMEM),
        scratch_shapes=[
            pltpu.VMEM((3, PIX, C1), BF16),
            pltpu.VMEM((PIX, C1), BF16),
            pltpu.VMEM((9, C1, C1), BF16),
            pltpu.VMEM((1, C1), F32),
            pltpu.SemaphoreType.DMA((3,)),
        ],
        compiler_params=pltpu.CompilerParams(vmem_limit_bytes=12 * 2**20),
        cost_estimate=pl.CostEstimate(
            flops=300_000_000, bytes_accessed=1_500_000, transcendentals=0
        ),
        name="conv_work",
    )(x, w1, bias)


def boxes_work(cot, w2):
    return pl.pallas_call(
        boxes_body,
        out_shape=(
            jax.ShapeDtypeStruct((PIX, 9 * C2), BF16),
            jax.ShapeDtypeStruct((PIX, C1), F32),
            jax.ShapeDtypeStruct((6, C1, C2), BF16),
        ),
        in_specs=[VMEM, HBM],
        out_specs=(VMEM, VMEM, VMEM),
        scratch_shapes=[pltpu.VMEM((9, C1, C2), BF16), pltpu.SemaphoreType.DMA],
        compiler_params=pltpu.CompilerParams(vmem_limit_bytes=12 * 2**20),
        cost_estimate=pl.CostEstimate(
            flops=300_000_000, bytes_accessed=1_500_000, transcendentals=0
        ),
        name="boxes_work",
    )(cot, w2)


def main_work(code, above, below, cot, preact, boxes, grad_act, w1_edge, w2_edge, x):
    return pl.pallas_call(
        main_body,
        out_shape=(
            jax.ShapeDtypeStruct((PIX, C1), BF16),
            jax.ShapeDtypeStruct((COLS, C1), BF16),
            jax.ShapeDtypeStruct((COLS, C1), BF16),
            jax.ShapeDtypeStruct((2,) + PARTS, BF16),
            jax.ShapeDtypeStruct(PARTS, BF16),
        ),
        in_specs=[SMEM] + [VMEM] * 8 + [HBM],
        out_specs=(VMEM, VMEM, VMEM, VMEM, ANYWHERE),
        scratch_shapes=[
            pltpu.VMEM((PIX + 2 * COLS, C1), BF16),
            pltpu.VMEM((PIX, 9 * C2), BF16),
            pltpu.VMEM((3, PIX, C1), BF16),
            pltpu.VMEM((PIX, C1), F32),
            pltpu.VMEM((PIX, C1), F32),
            pltpu.SemaphoreType.DMA((2,)),
        ],
        compiler_params=pltpu.CompilerParams(vmem_limit_bytes=16 * 2**20),
        cost_estimate=pl.CostEstimate(
            flops=600_000_000, bytes_accessed=5_000_000, transcendentals=70_000
        ),
        name="main_work",
    )(code, above, below, cot, preact, boxes, grad_act, w1_edge, w2_edge, x)


def pair_body(code, packed, received, pair, total, sems):
    mine = code[0] % 2
    copies = []
    for n in range(4):
        chunks = pl.ds(n * (CHUNK // 4), CHUNK // 4)
        total[chunks] = packed[mine, chunks] + received[chunks]
        copies.append(start(total.at[chunks], pair.at[chunks], sems.at[n]))
    for copy in copies:
        copy.wait()


def pair_work(code, packed, received):
    return pl.pallas_call(
        pair_body,
        out_shape=jax.ShapeDtypeStruct(PARTS, BF16),
        in_specs=[SMEM, VMEM, VMEM],
        out_specs=ANYWHERE,
        scratch_shapes=[pltpu.VMEM(PARTS, BF16), pltpu.SemaphoreType.DMA((4,))],
        compiler_params=pltpu.CompilerParams(vmem_limit_bytes=8 * 2**20),
        name="pair_work",
    )(code, packed, received)


def block_body(code, pieces, out, total):
    value = pieces[0].astype(F32)
    for n in range(1, 32):
        value = value + pieces[n].astype(F32)
    tiles = CHUNK // 16
    total[0:tiles] = value.reshape(tiles, 16, 128)
    total[tiles] = jnp.zeros((16, 128), F32)
    single = code[0] // 2 % 4
    for z_hi in range(4):
        part = total[pl.ds(2 * z_hi - jnp.where(z_hi > single, 1, 0), 2)]
        for n, (target, _) in enumerate(Z_ORDER):
            if target == z_hi:
                out[n] = part.reshape(PIECE).astype(BF16)


def block_work(code, pieces):
    return pl.pallas_call(
        block_body,
        out_shape=jax.ShapeDtypeStruct((8,) + PIECE, BF16),
        in_specs=[SMEM, VMEM],
        out_specs=VMEM,
        scratch_shapes=[pltpu.VMEM((TILES // 4 + 1, 16, 128), F32)],
        compiler_params=pltpu.CompilerParams(vmem_limit_bytes=4 * 2**20),
        name="block_work",
    )(code, pieces)


def column_body(pieces, out):
    total = pieces[0].astype(F32)
    for n in range(1, pieces.shape[0]):
        total = total + pieces[n].astype(F32)
    for n in range(PIECES):
        out[n] = total.astype(BF16)


def column_work(pieces):
    return pl.pallas_call(
        column_body,
        out_shape=jax.ShapeDtypeStruct((PIECES,) + PIECE, BF16),
        in_specs=[VMEM],
        out_specs=VMEM,
        compiler_params=pltpu.CompilerParams(vmem_limit_bytes=4 * 2**20),
        name="column_work",
    )(pieces)


def input_body(delta, above, below, w1_hbm, grad_x, ext, ds, w1, sem):
    w1_copy = pltpu.make_async_copy(w1_hbm, w1, sem)
    w1_copy.start()
    ext[0:COLS, :] = above[...]
    ext[COLS : COLS + PIX, :] = delta[...]
    ext[COLS + PIX :, :] = below[...]
    wide = ext[...].astype(F32)
    ds[0] = shifted(wide, 1).astype(BF16)
    ds[1] = ext[...]
    ds[2] = shifted(wide, -1).astype(BF16)
    w1_copy.wait()
    total = jnp.zeros((PIX, C1), F32)
    for p in range(3):
        for q in range(3):
            at = COLS * (2 - p)
            total = total + dot(ds[q, at : at + PIX, :], w1[3 * p + q], NT)
    grad_x[...] = total.astype(BF16)


def input_work(delta, above, below, w1):
    return pl.pallas_call(
        input_body,
        out_shape=jax.ShapeDtypeStruct((PIX, C1), BF16),
        in_specs=[VMEM] * 3 + [HBM],
        out_specs=VMEM,
        scratch_shapes=[
            pltpu.VMEM((PIX + 2 * COLS, C1), BF16),
            pltpu.VMEM((3, PIX + 2 * COLS, C1), BF16),
            pltpu.VMEM((9, C1, C1), BF16),
            pltpu.SemaphoreType.DMA,
        ],
        compiler_params=pltpu.CompilerParams(vmem_limit_bytes=12 * 2**20),
        cost_estimate=pl.CostEstimate(
            flops=300_000_000, bytes_accessed=2_000_000, transcendentals=0
        ),
        name="input_work",
    )(delta, above, below, w1)


def unpack(scale_low, scale_high, code, full, first, second, bias, tiles):
    z_hi = code[0] // 8
    for half in range(2):
        for k in range(8):
            before = 2 * k - (k - z_hi + 3) // 4
            piece = full[8 * half + k].astype(F32).reshape(2, 16, 128)
            tiles[pl.ds(half * (TILES // 2) + before, 2)] = piece

    def band(n):
        return tiles[9 * n : 9 * n + 9].reshape(SLICE, 128)

    first[:, 0:C2] = band(0) * scale_low
    first[:, C2:C1] = band(1) * scale_low
    second[...] = band(2) * scale_high
    bias[...] = tiles[TILES - 1][0:1, 0:16] * scale_low


def results(code, full, scale_low, scale_high):
    return pl.pallas_call(
        lambda *refs: unpack(scale_low, scale_high, *refs),
        out_shape=(
            jax.ShapeDtypeStruct((SLICE, C1), F32),
            jax.ShapeDtypeStruct((SLICE, C2), F32),
            jax.ShapeDtypeStruct((1, 16), F32),
        ),
        in_specs=[SMEM, VMEM],
        out_specs=(VMEM,) * 3,
        scratch_shapes=[pltpu.VMEM((TILES + 1, 16, 128), F32)],
        name="unpack",
    )(code, full)


FOUR = range(4)
TWO = range(2)


def place(x, z_hi, y, zb, za, core):
    return (x * 4 + z_hi) * 32 + y * 8 + zb * 4 + za * 2 + core


BLOCK = [
    [place(n // 8, zh, n // 2 % 4, zb, n % 2, c) for n in ORDER]
    for zh in FOUR
    for zb in TWO
    for c in TWO
]
Z_ORDER = [(0, 0), (2, 0), (0, 1), (2, 1), (1, 0), (3, 0), (1, 1), (3, 1)]
COLUMN = [
    [place(x, zh, y, zb, za, c) for zh, zb in Z_ORDER]
    for x in FOUR
    for y in FOUR
    for za in TWO
    for c in TWO
]
SHARE = [[place(0, 0, y, zb, za, c) for c in TWO for y in FOUR for za in TWO] for zb in TWO]
QUADS = [[4 * j + b for b in FOUR] for j in range(8)]


def shards(cotangent, inputs, w_first, bias_first, w_second):
    rank = lax.axis_index("rows")
    down = [(i, i + 4) for i in range(28)]
    up = [(i + 4, i) for i in range(28)]
    both = ("dp", "rows")
    x = inputs[0]

    cot = lax.all_to_all(cotangent, "rows", 0, 0, axis_index_groups=QUADS)
    cot = cot.reshape(8, 128, C2)

    def halo(cot_rows, x_row):
        row = jnp.concatenate([x_row[:, :C2], x_row[:, C2:]], axis=0)
        return jnp.concatenate([cot_rows, row[None]])

    above = lax.ppermute(halo(cot[7:8], x[3]), "rows", down)
    below = lax.ppermute(halo(cot[0:1], x[0]), "rows", up)
    code = rank % 2 + rank // 2 % 2 * 2 + rank // 8 % 2 * 4 + lax.axis_index("dp") % 4 * 8
    code = code.astype(jnp.int32).reshape(1)
    x_flat, w1, bias, w2 = (
        pltpu.with_memory_space_constraint(value, pltpu.HBM)
        for value in (
            x.reshape(PIX, C1),
            w_first.reshape(9, C1, C1),
            bias_first.reshape(1, C1),
            w_second.reshape(9, C1, C2),
        )
    )
    cot = cot.reshape(8 * 128, C2)
    preact, w1_edge = conv_work(x_flat, w1, bias)
    boxes, grad_act, w2_edge = boxes_work(cot, w2)
    delta, delta_first, delta_last, packed, send = main_work(
        code, above, below, cot, preact, boxes, grad_act, w1_edge, w2_edge, x_flat
    )
    received = lax.ppermute(send, "rows", [(i, i ^ 1) for i in range(32)])
    from_above = lax.ppermute(delta_last, "rows", down)
    from_below = lax.ppermute(delta_first, "rows", up)

    pair = pair_work(code, packed, received)
    pair = pair.reshape(32, CHUNK, 128)
    block = lax.all_to_all(pair, both, 0, 0, axis_index_groups=BLOCK)
    block, from_above, from_below = lax.optimization_barrier((block, from_above, from_below))
    spread = block_work(code, block)
    column = lax.all_to_all(spread, both, 0, 0, axis_index_groups=COLUMN)
    column, delta = lax.optimization_barrier((column, delta))
    grad_x = input_work(delta, from_above, from_below, w1)
    full = lax.all_to_all(column_work(column), "rows", 0, 0, axis_index_groups=SHARE)

    pixels_low = lax.axis_size("dp") * lax.axis_size("rows") * PIX
    scale_low = pixels_low ** (-0.5)
    scale_high = (4 * pixels_low) ** (-0.5)
    full, grad_x = lax.optimization_barrier((full, grad_x))
    full = pltpu.with_memory_space_constraint(full, pltpu.VMEM)
    grad_first, grad_second, grad_bias = results(code, full, scale_low, scale_high)
    grad_input = grad_x.reshape(1, ROWS, COLS, C1)
    return grad_input, grad_first, grad_second, grad_bias.reshape(16)


def solution(mesh):
    in_specs = (P("dp", "rows", None, None), P("dp", "rows", None, None), P(), P(), P())
    out_specs = (P("dp", "rows", None, None), P("dp", None), P("dp", None), P("dp"))
    return jax.shard_map(shards, mesh=mesh, in_specs=in_specs, out_specs=out_specs, check_vma=False)
```

```python
import jax
import jax.numpy as jnp
from jax import lax
from jax.experimental import pallas as pl
from jax.experimental.pallas import tpu as pltpu
from jax.sharding import PartitionSpec as P

F32 = jnp.float32
BF16 = jnp.bfloat16
COLS = 64
C1 = 256
C2 = 128
ROWS = 4
PIX = ROWS * COLS
SLICE = 144
TILES = 28
PIECE = (32, 128)
PIECES = 16
ORDER = [
    26, 17, 11, 10, 28, 1, 5, 4, 7, 16, 9, 19, 30, 13, 22, 0,
    21, 29, 6, 12, 20, 23, 14, 15, 3, 31, 2, 24, 25, 27, 18, 8,
]
CHUNK = 16 * TILES // 4
PARTS = (CHUNK, 32, 128)


def dot(a, b, contract):
    return lax.dot_general(a, b, (contract, ((), ())), preferred_element_type=F32)


NN = ((1,), (0,))
NT = ((1,), (1,))
TN = ((0,), (0,))


def shifted(value, by):
    length = value.shape[0]
    column = lax.broadcasted_iota(jnp.int32, value.shape, 0) % COLS
    rolled = pltpu.roll(value, (-by) % length, 0)
    inside = (column + by >= 0) & (column + by < COLS)
    return jnp.where(inside, rolled, 0.0)


def tiles_of(k, z_hi):
    return 1 if k % 4 == z_hi else 2


def spot(d, tile):
    half, tile = divmod(tile, TILES // 2)
    x, z_hi = divmod(d, 4)
    k = 0
    while tile >= tiles_of(k, z_hi):
        tile -= tiles_of(k, z_hi)
        k += 1
    before = sum(tiles_of(k, z) for z in range(z_hi)) + tile
    return half, CHUNK * ORDER.index(x * 8 + k) + 16 * before


def put(packed, band, tap, value):
    for row in range(0, C1, 16):
        d, inner = divmod(tap * C1 + row, SLICE)
        half, at = spot(d, band * (SLICE // 16) + inner // 16)
        packed[half, at // 32, at % 32 : at % 32 + 16, :] = value[row : row + 16, :]


def pick_columns():
    out_row = lax.broadcasted_iota(jnp.int32, (3 * COLS, 256), 0)
    column = lax.broadcasted_iota(jnp.int32, (3 * COLS, 256), 1) % 128
    left = 2 * (out_row % COLS) + 1 - out_row // COLS
    return ((column == left) | (column == left + 1)).astype(F32).astype(BF16)


def silu_parts(preact):
    sigma = 1.0 / (1.0 + jnp.exp(-preact))
    return preact * sigma, sigma * (1.0 + preact * (1.0 - sigma))


def start(source, target, sem):
    copy = pltpu.make_async_copy(source, target, sem)
    copy.start()
    return copy


def conv_body(x_hbm, w1_hbm, bias_hbm, preact, w1_edge, xs, x, w1, bias, sems):
    x_copy = start(x_hbm, x, sems.at[0])
    bias_copy = start(bias_hbm, bias, sems.at[1])
    w1_copy = start(w1_hbm, w1, sems.at[2])
    x_copy.wait()
    wide = x[...].astype(F32)
    xs[0] = shifted(wide, -1).astype(BF16)
    xs[1] = x[...]
    xs[2] = shifted(wide, 1).astype(BF16)
    bias_copy.wait()
    w1_copy.wait()
    same = jnp.broadcast_to(bias[...], (PIX, C1))
    lower = jnp.zeros((PIX - COLS, C1), F32)
    upper = jnp.zeros((PIX - COLS, C1), F32)
    for q in range(3):
        lower = lower + dot(xs[q, 0 : PIX - COLS, :], w1[q], NN)
        same = same + dot(xs[q], w1[3 + q], NN)
        upper = upper + dot(xs[q, COLS:PIX, :], w1[6 + q], NN)
    preact[0:COLS, :] = same[0:COLS] + upper[0:COLS]
    middle = slice(COLS, PIX - COLS)
    preact[middle, :] = same[middle] + upper[COLS:] + lower[: PIX - 2 * COLS]
    preact[PIX - COLS :, :] = same[PIX - COLS :] + lower[PIX - 2 * COLS :]
    w1_edge[0:3] = w1[0:3]
    w1_edge[3:6] = w1[6:9]


def boxes_body(cot, w2_hbm, boxes, grad_act, w2_edge, w2, sem):
    w2_copy = start(w2_hbm, w2, sem)
    pick = pick_columns()
    zero = jnp.zeros((COLS, 3 * C2), BF16)
    boxes[0:COLS, 6 * C2 :] = zero
    boxes[PIX - COLS :, 0 : 3 * C2] = zero
    for h in range(7):
        sums = dot(pick, cot[128 * h : 128 * (h + 2), :], NN).astype(BF16)
        for p in range(3):
            if (h + p - 1) % 2 == 0 and 0 <= (h + p - 1) // 2 < ROWS:
                i = (h + p - 1) // 2
                for q in range(3):
                    t = 3 * p + q
                    boxes[COLS * i : COLS * (i + 1), C2 * t : C2 * (t + 1)] = sums[
                        COLS * q : COLS * (q + 1), :
                    ]
    w2_copy.wait()
    total = jnp.zeros((PIX, C1), F32)
    for t in range(9):
        total = total + dot(boxes[:, C2 * t : C2 * (t + 1)], w2[t], NT)
    grad_act[...] = total
    w2_edge[0:3] = w2[6:9]
    w2_edge[3:6] = w2[0:3]


def main_body(
    code, above, below, cot, preact_in, boxes_in, grad_act_in, w1_edge, w2_edge, x_hbm,
    delta_out, delta_first, delta_last, packed, send,
    x, boxes, ds, preact, grad_act, sems,
):
    x_copy = start(x_hbm, x.at[COLS : COLS + PIX], sems.at[1])

    boxes[...] = boxes_in[...]
    grad_act[...] = grad_act_in[...]
    preact[...] = preact_in[...]
    pick = pick_columns()
    first, last = slice(0, COLS), slice(PIX - COLS, PIX)
    for rows, p, pair in (
        (first, 2, (above[0], cot[0:128, :])),
        (last, 0, (cot[128 * 7 : 128 * 8, :], below[0])),
    ):
        sums = dot(pick, jnp.concatenate(pair), NN).astype(BF16)
        for q in range(3):
            t = 3 * p + q
            boxes[rows, C2 * t : C2 * (t + 1)] = sums[COLS * q : COLS * (q + 1), :]
    for at, halo in ((0, above), (COLS + PIX, below)):
        x[at : at + COLS, 0:C2] = halo[1, 0:COLS, :]
        x[at : at + COLS, C2:C1] = halo[1, COLS : 2 * COLS, :]
    for side, rows, p in ((0, first, 2), (1, last, 0)):
        part = grad_act[rows, :]
        for q in range(3):
            t = 3 * p + q
            part = part + dot(boxes[rows, C2 * t : C2 * (t + 1)], w2_edge[3 * side + q], NT)
        grad_act[rows, :] = part
    for side, rows, at in ((0, first, 0), (1, last, COLS + PIX)):
        wide = x[at : at + COLS, :].astype(F32)
        part = preact[rows, :]
        for q in range(3):
            part = part + dot(shifted(wide, q - 1).astype(BF16), w1_edge[3 * side + q], NN)
        preact[rows, :] = part
    act, slope = silu_parts(preact[...])
    second = dot(act.astype(BF16), boxes[...], TN).astype(BF16)
    for t in range(9):
        put(packed, 2, t, second[:, C2 * t : C2 * (t + 1)])

    delta = (grad_act[...] * slope).astype(BF16)
    delta_out[...] = delta
    delta_first[...] = delta[0:COLS]
    delta_last[...] = delta[PIX - COLS : PIX]
    wide = delta.astype(F32)
    ds[0] = shifted(wide, 1).astype(BF16)
    ds[1] = delta
    ds[2] = shifted(wide, -1).astype(BF16)

    total = jnp.sum(wide, axis=0, keepdims=True).astype(BF16).astype(F32)
    owner = lax.broadcasted_iota(jnp.int32, (16, C1), 0)
    channel = lax.broadcasted_iota(jnp.int32, (16, C1), 1)
    spread = jnp.where(channel // 16 == owner, jnp.broadcast_to(total, (16, C1)), 0.0)
    source = lax.broadcasted_iota(jnp.int32, (C1, 128), 0)
    lane = lax.broadcasted_iota(jnp.int32, (C1, 128), 1)
    fold = (source % 16 == lane).astype(F32).astype(BF16)
    folded = dot(spread.astype(BF16), fold, NN)
    row = lax.broadcasted_iota(jnp.int32, (16, 16, 128), 1)
    band = jnp.where(row == 0, jnp.broadcast_to(folded[:, None, :], (16, 16, 128)), 0.0)
    band = band.astype(BF16)
    for d in range(16):
        half, at = spot(d, TILES - 1)
        packed[half, at // 32, at % 32 : at % 32 + 16, :] = band[d]

    x_copy.wait()
    for p in range(3):
        lhs = x[p * COLS : p * COLS + PIX, :]
        for q in range(3):
            tap = 3 * p + q
            part = dot(lhs, ds[q], TN).astype(BF16)
            put(packed, 0, tap, part[:, 0:C2])
            put(packed, 1, tap, part[:, C2:C1])
    start(packed.at[1 - code[0] % 2], send, sems.at[0]).wait()


VMEM = pl.BlockSpec(memory_space=pltpu.VMEM)
HBM = pl.BlockSpec(memory_space=pltpu.HBM)
SMEM = pl.BlockSpec(memory_space=pltpu.SMEM)
ANYWHERE = pl.BlockSpec(memory_space=pl.ANY)


def conv_work(x, w1, bias):
    return pl.pallas_call(
        conv_body,
        out_shape=(
            jax.ShapeDtypeStruct((PIX, C1), F32),
            jax.ShapeDtypeStruct((6, C1, C1), BF16),
        ),
        in_specs=[HBM] * 3,
        out_specs=(VMEM, VMEM),
        scratch_shapes=[
            pltpu.VMEM((3, PIX, C1), BF16),
            pltpu.VMEM((PIX, C1), BF16),
            pltpu.VMEM((9, C1, C1), BF16),
            pltpu.VMEM((1, C1), F32),
            pltpu.SemaphoreType.DMA((3,)),
        ],
        compiler_params=pltpu.CompilerParams(vmem_limit_bytes=12 * 2**20),
        cost_estimate=pl.CostEstimate(
            flops=300_000_000, bytes_accessed=1_500_000, transcendentals=0
        ),
        name="conv_work",
    )(x, w1, bias)


def boxes_work(cot, w2):
    return pl.pallas_call(
        boxes_body,
        out_shape=(
            jax.ShapeDtypeStruct((PIX, 9 * C2), BF16),
            jax.ShapeDtypeStruct((PIX, C1), F32),
            jax.ShapeDtypeStruct((6, C1, C2), BF16),
        ),
        in_specs=[VMEM, HBM],
        out_specs=(VMEM, VMEM, VMEM),
        scratch_shapes=[pltpu.VMEM((9, C1, C2), BF16), pltpu.SemaphoreType.DMA],
        compiler_params=pltpu.CompilerParams(vmem_limit_bytes=12 * 2**20),
        cost_estimate=pl.CostEstimate(
            flops=300_000_000, bytes_accessed=1_500_000, transcendentals=0
        ),
        name="boxes_work",
    )(cot, w2)


def main_work(code, above, below, cot, preact, boxes, grad_act, w1_edge, w2_edge, x):
    return pl.pallas_call(
        main_body,
        out_shape=(
            jax.ShapeDtypeStruct((PIX, C1), BF16),
            jax.ShapeDtypeStruct((COLS, C1), BF16),
            jax.ShapeDtypeStruct((COLS, C1), BF16),
            jax.ShapeDtypeStruct((2,) + PARTS, BF16),
            jax.ShapeDtypeStruct(PARTS, BF16),
        ),
        in_specs=[SMEM] + [VMEM] * 8 + [HBM],
        out_specs=(VMEM, VMEM, VMEM, VMEM, ANYWHERE),
        scratch_shapes=[
            pltpu.VMEM((PIX + 2 * COLS, C1), BF16),
            pltpu.VMEM((PIX, 9 * C2), BF16),
            pltpu.VMEM((3, PIX, C1), BF16),
            pltpu.VMEM((PIX, C1), F32),
            pltpu.VMEM((PIX, C1), F32),
            pltpu.SemaphoreType.DMA((2,)),
        ],
        compiler_params=pltpu.CompilerParams(vmem_limit_bytes=16 * 2**20),
        cost_estimate=pl.CostEstimate(
            flops=600_000_000, bytes_accessed=5_000_000, transcendentals=70_000
        ),
        name="main_work",
    )(code, above, below, cot, preact, boxes, grad_act, w1_edge, w2_edge, x)


def pair_body(code, packed, received, pair, total, sems):
    mine = code[0] % 2
    copies = []
    for n in range(4):
        chunks = pl.ds(n * (CHUNK // 4), CHUNK // 4)
        total[chunks] = packed[mine, chunks] + received[chunks]
        copies.append(start(total.at[chunks], pair.at[chunks], sems.at[n]))
    for copy in copies:
        copy.wait()


def pair_work(code, packed, received):
    return pl.pallas_call(
        pair_body,
        out_shape=jax.ShapeDtypeStruct(PARTS, BF16),
        in_specs=[SMEM, VMEM, VMEM],
        out_specs=ANYWHERE,
        scratch_shapes=[pltpu.VMEM(PARTS, BF16), pltpu.SemaphoreType.DMA((4,))],
        compiler_params=pltpu.CompilerParams(vmem_limit_bytes=8 * 2**20),
        name="pair_work",
    )(code, packed, received)


def block_body(code, pieces, out, total):
    value = pieces[0].astype(F32)
    for n in range(1, 32):
        value = value + pieces[n].astype(F32)
    tiles = CHUNK // 16
    total[0:tiles] = value.reshape(tiles, 16, 128)
    total[tiles] = jnp.zeros((16, 128), F32)
    single = code[0] // 2 % 4
    for z_hi in range(4):
        part = total[pl.ds(2 * z_hi - jnp.where(z_hi > single, 1, 0), 2)]
        for n, (target, _) in enumerate(Z_ORDER):
            if target == z_hi:
                out[n] = part.reshape(PIECE).astype(BF16)


def block_work(code, pieces):
    return pl.pallas_call(
        block_body,
        out_shape=jax.ShapeDtypeStruct((8,) + PIECE, BF16),
        in_specs=[SMEM, VMEM],
        out_specs=VMEM,
        scratch_shapes=[pltpu.VMEM((TILES // 4 + 1, 16, 128), F32)],
        compiler_params=pltpu.CompilerParams(vmem_limit_bytes=4 * 2**20),
        name="block_work",
    )(code, pieces)


def column_body(pieces, out):
    total = pieces[0].astype(F32)
    for n in range(1, pieces.shape[0]):
        total = total + pieces[n].astype(F32)
    for n in range(PIECES):
        out[n] = total.astype(BF16)


def column_work(pieces):
    return pl.pallas_call(
        column_body,
        out_shape=jax.ShapeDtypeStruct((PIECES,) + PIECE, BF16),
        in_specs=[VMEM],
        out_specs=VMEM,
        compiler_params=pltpu.CompilerParams(vmem_limit_bytes=4 * 2**20),
        name="column_work",
    )(pieces)


def input_body(delta, above, below, w1_hbm, grad_x, ext, ds, w1, sem):
    w1_copy = pltpu.make_async_copy(w1_hbm, w1, sem)
    w1_copy.start()
    ext[0:COLS, :] = above[...]
    ext[COLS : COLS + PIX, :] = delta[...]
    ext[COLS + PIX :, :] = below[...]
    wide = ext[...].astype(F32)
    ds[0] = shifted(wide, 1).astype(BF16)
    ds[1] = ext[...]
    ds[2] = shifted(wide, -1).astype(BF16)
    w1_copy.wait()
    total = jnp.zeros((PIX, C1), F32)
    for p in range(3):
        for q in range(3):
            at = COLS * (2 - p)
            total = total + dot(ds[q, at : at + PIX, :], w1[3 * p + q], NT)
    grad_x[...] = total.astype(BF16)


def input_work(delta, above, below, w1):
    return pl.pallas_call(
        input_body,
        out_shape=jax.ShapeDtypeStruct((PIX, C1), BF16),
        in_specs=[VMEM] * 3 + [HBM],
        out_specs=VMEM,
        scratch_shapes=[
            pltpu.VMEM((PIX + 2 * COLS, C1), BF16),
            pltpu.VMEM((3, PIX + 2 * COLS, C1), BF16),
            pltpu.VMEM((9, C1, C1), BF16),
            pltpu.SemaphoreType.DMA,
        ],
        compiler_params=pltpu.CompilerParams(vmem_limit_bytes=12 * 2**20),
        cost_estimate=pl.CostEstimate(
            flops=300_000_000, bytes_accessed=2_000_000, transcendentals=0
        ),
        name="input_work",
    )(delta, above, below, w1)


def unpack(scale_low, scale_high, code, full, first, second, bias, tiles):
    z_hi = code[0] // 8
    for half in range(2):
        for k in range(8):
            before = 2 * k - (k - z_hi + 3) // 4
            piece = full[2 * k + half].astype(F32).reshape(2, 16, 128)
            tiles[pl.ds(half * (TILES // 2) + before, 2)] = piece

    def band(n):
        return tiles[9 * n : 9 * n + 9].reshape(SLICE, 128)

    first[:, 0:C2] = band(0) * scale_low
    first[:, C2:C1] = band(1) * scale_low
    second[...] = band(2) * scale_high
    bias[...] = tiles[TILES - 1][0:1, 0:16] * scale_low


def results(code, full, scale_low, scale_high):
    return pl.pallas_call(
        lambda *refs: unpack(scale_low, scale_high, *refs),
        out_shape=(
            jax.ShapeDtypeStruct((SLICE, C1), F32),
            jax.ShapeDtypeStruct((SLICE, C2), F32),
            jax.ShapeDtypeStruct((1, 16), F32),
        ),
        in_specs=[SMEM, VMEM],
        out_specs=(VMEM,) * 3,
        scratch_shapes=[pltpu.VMEM((TILES + 1, 16, 128), F32)],
        name="unpack",
    )(code, full)


FOUR = range(4)
TWO = range(2)


def place(x, z_hi, y, zb, za, core):
    return (x * 4 + z_hi) * 32 + y * 8 + zb * 4 + za * 2 + core


BLOCK = [
    [place(n // 8, zh, n // 2 % 4, zb, n % 2, c) for n in ORDER]
    for zh in FOUR
    for zb in TWO
    for c in TWO
]
Z_ORDER = [(0, 0), (2, 0), (0, 1), (2, 1), (1, 0), (3, 0), (1, 1), (3, 1)]
COLUMN = [
    [place(x, zh, y, zb, za, c) for zh, zb in Z_ORDER]
    for x in FOUR
    for y in FOUR
    for za in TWO
    for c in TWO
]
SHARE = [[place(0, 0, y, zb, za, c) for y in FOUR for za in TWO for c in TWO] for zb in TWO]
QUADS = [[4 * j + b for b in FOUR] for j in range(8)]


def shards(cotangent, inputs, w_first, bias_first, w_second):
    rank = lax.axis_index("rows")
    down = [(i, i + 4) for i in range(28)]
    up = [(i + 4, i) for i in range(28)]
    both = ("dp", "rows")
    x = inputs[0]

    cot = lax.all_to_all(cotangent, "rows", 0, 0, axis_index_groups=QUADS)
    cot = cot.reshape(8, 128, C2)

    def halo(cot_rows, x_row):
        row = jnp.concatenate([x_row[:, :C2], x_row[:, C2:]], axis=0)
        return jnp.concatenate([cot_rows, row[None]])

    above = lax.ppermute(halo(cot[7:8], x[3]), "rows", down)
    below = lax.ppermute(halo(cot[0:1], x[0]), "rows", up)
    code = rank % 2 + rank // 2 % 2 * 2 + rank // 8 % 2 * 4 + lax.axis_index("dp") % 4 * 8
    code = code.astype(jnp.int32).reshape(1)
    x_flat, w1, bias, w2 = (
        pltpu.with_memory_space_constraint(value, pltpu.HBM)
        for value in (
            x.reshape(PIX, C1),
            w_first.reshape(9, C1, C1),
            bias_first.reshape(1, C1),
            w_second.reshape(9, C1, C2),
        )
    )
    cot = cot.reshape(8 * 128, C2)
    preact, w1_edge = conv_work(x_flat, w1, bias)
    boxes, grad_act, w2_edge = boxes_work(cot, w2)
    delta, delta_first, delta_last, packed, send = main_work(
        code, above, below, cot, preact, boxes, grad_act, w1_edge, w2_edge, x_flat
    )
    received = lax.ppermute(send, "rows", [(i, i ^ 1) for i in range(32)])
    from_above = lax.ppermute(delta_last, "rows", down)
    from_below = lax.ppermute(delta_first, "rows", up)

    pair = pair_work(code, packed, received)
    pair = pair.reshape(32, CHUNK, 128)
    block = lax.all_to_all(pair, both, 0, 0, axis_index_groups=BLOCK)
    block, from_above, from_below = lax.optimization_barrier((block, from_above, from_below))
    grad_x = input_work(delta, from_above, from_below, w1)
    spread = block_work(code, block)
    column = lax.all_to_all(spread, both, 0, 0, axis_index_groups=COLUMN)
    column, grad_x = lax.optimization_barrier((column, grad_x))
    full = lax.all_to_all(column_work(column), "rows", 0, 0, axis_index_groups=SHARE)

    pixels_low = lax.axis_size("dp") * lax.axis_size("rows") * PIX
    scale_low = pixels_low ** (-0.5)
    scale_high = (4 * pixels_low) ** (-0.5)
    full = pltpu.with_memory_space_constraint(full, pltpu.VMEM)
    grad_first, grad_second, grad_bias = results(code, full, scale_low, scale_high)
    grad_input = grad_x.reshape(1, ROWS, COLS, C1)
    return grad_input, grad_first, grad_second, grad_bias.reshape(16)


def solution(mesh):
    in_specs = (P("dp", "rows", None, None), P("dp", "rows", None, None), P(), P(), P())
    out_specs = (P("dp", "rows", None, None), P("dp", None), P("dp", None), P("dp"))
    return jax.shard_map(shards, mesh=mesh, in_specs=in_specs, out_specs=out_specs, check_vma=False)
```
